32 devices in a mesh: feat: 16 (over z, y, x), rows: 2 (over core).
Axes of the slice: x: 2, y: 2, z: 4, core: 2. Of those that a mesh axis runs over, the one named last changes fastest.
Arguments:
- embeddings: bfloat16 [256, 512], P('rows'), may hold values from -6 to 6
- sign_flips: float32 [524288], P('feat'), may hold values from -1 to 1, as said below
- gaussian: float32 [524288], P('feat'), may hold values from -5 to 5
- scales: float32 [524288], P('feat'), may hold values from 0.5 to 2
- phases: float32 [524288], P('feat'), may hold values from 0 to 6.2831855
- source_blocks: int32 [4096], P('feat'), may hold values from 0 to 4095, as said below
- block_permutations: bfloat16 [4096, 128, 128], P('feat'), may hold values from 0 to 1, as said below
- weights: float32 [524288], P('feat'), may hold values from -6 to 6
- targets: float32 [256], P('rows'), may hold values from -6 to 6
Outputs:
- predictions: float32 [256], P('rows')
- feature_grad: float32 [524288], P(('feat', 'rows'))
The draws below stay inside these ranges and needn't reach their ends.
Inputs may be any that keep to these rules, and one draw needn't show every extreme that they name: `sign_flips`: each entry is -1 or 1. `source_blocks`: A permutation of the 4096 block numbers. The 256 entries of each aligned run of 256 entries name exactly 16 blocks from every aligned run of 256 blocks. Each block_permutations[b] is a permutation matrix.
All inputs are finite; a program needn't handle non-finite values.
Results may differ from the reference program's by a relative error of at most 0.0003.
Values sent between devices are 32-bit elements; how exact they have to be, the bound alone decides.
No kernel may reach another device: no remote copies, remote signals or barrier semaphores. Data moves between devices by JAX's collectives and lax.ppermute only.
A program may use at most 128 MiB of HBM per device.

```python
import math
import jax
import jax.numpy as jnp
from jax import lax

D = 512
FEATURE_COUNT = 524288
BLOCK = 128
ROWS = 256
BLOCKS = 4096
BLK_DEV = 256
FEAT_SHARDS = 16


def draw_sign_flips(key, part):
    return jax.random.rademacher(jax.random.fold_in(key, 11), (FEATURE_COUNT,), dtype=jnp.float32)


def draw_source_blocks(key, part):
    device_shards = FEAT_SHARDS
    local_count = BLK_DEV
    primary_key = jax.random.fold_in(key, 21)
    second_key = jax.random.fold_in(key, 22)
    dest_perm = jax.vmap(lambda k: jax.random.permutation(k, local_count))(jax.random.split(primary_key, device_shards))
    source_perm = jax.vmap(lambda k: jax.random.permutation(k, local_count))(jax.random.split(second_key, device_shards))
    target_index = jnp.arange(device_shards, dtype=jnp.int32)[:, None]
    quotient = dest_perm // device_shards
    remainder = dest_perm % device_shards
    source_dev = (target_index + remainder) % device_shards
    source_local = source_perm[source_dev, quotient * device_shards + remainder]
    table = source_dev * local_count + source_local
    return table.reshape(-1).astype(jnp.int32)


def draw_block_permutations(key, part):
    keys = jax.random.split(jax.random.fold_in(key, 31), BLOCKS)
    orders = jax.vmap(lambda k: jax.random.permutation(k, BLOCK))(keys)
    return jax.nn.one_hot(orders, BLOCK, dtype=jnp.float32).astype(jnp.bfloat16)


def shard_levels(rng, shape, pieces, smallest, largest):
    gain = 1.0
    for dim, blocks in pieces:
        heights = jax.random.uniform(jax.random.fold_in(jax.random.fold_in(rng, 6), dim), (blocks,), jnp.float32, smallest / len(pieces), largest / len(pieces))
        gain = gain * jnp.repeat(jnp.exp(heights), shape[dim] // blocks).reshape((-1,) + (1,) * (len(shape) - 1 - dim))
    return gain


def scatter_about(rng, dims, scale, bound, cuts=(), held_as=jnp.bfloat16):
    values = jax.random.normal(rng, dims, jnp.float32) * scale
    if len(cuts) > 0:
        values = shard_levels(rng, dims, cuts, -0.22, 0.18) * values
    return jnp.clip(values, min=-bound, max=bound).astype(held_as)


def setup_inputs(seed: int = 0) -> dict:
    streams_of = jax.random.split(jax.random.key(seed), 10)
    return {
        "embeddings": scatter_about(streams_of[0], (ROWS, D), 1.0, 6.0, ((0, 2),)),
        "sign_flips": draw_sign_flips(jax.random.fold_in(streams_of[9], 71), 0),
        "gaussian": scatter_about(streams_of[2], (FEATURE_COUNT,), 1.0, 5.0, ((0, 16),), jnp.float32),
        "scales": jnp.clip(jnp.exp(math.log(2.0) - 1.3862944 * jax.random.uniform(streams_of[3], (FEATURE_COUNT,), jnp.float32) ** shard_levels(streams_of[3], (FEATURE_COUNT,), ((0, 16),), -0.2, 0.2)), 0.5, 2.0),
        "phases": jnp.clip(6.2831855 * jax.random.uniform(streams_of[4], (FEATURE_COUNT,), jnp.float32) ** shard_levels(streams_of[4], (FEATURE_COUNT,), ((0, 16),), -0.2, 0.2), 0.0, 6.2831855),
        "source_blocks": draw_source_blocks(jax.random.fold_in(streams_of[9], 71), 0),
        "block_permutations": draw_block_permutations(jax.random.fold_in(streams_of[9], 71), 0),
        "weights": scatter_about(streams_of[7], (FEATURE_COUNT,), 1.0, 6.0, ((0, 16),), jnp.float32),
        "targets": scatter_about(streams_of[8], (ROWS,), 1.0, 6.0, ((0, 2),), jnp.float32),
    }


def walsh(field):
    row_count = field.shape[0]
    length = field.shape[1]
    butterfly_half_width = 1
    while butterfly_half_width < length:
        shaped = field.reshape(row_count, length // (2 * butterfly_half_width), 2, butterfly_half_width)
        upper_half = shaped[:, :, 0, :]
        lower_half = shaped[:, :, 1, :]
        field = jnp.stack([upper_half + lower_half, upper_half - lower_half], axis=2).reshape(row_count, length)
        butterfly_half_width = butterfly_half_width * 2
    return field * (1.0 / math.sqrt(FEATURE_COUNT))

def reference(embeddings, sign_flips, gaussian, scales, phases, source_blocks, block_permutations, weights, targets):
    tiled = jnp.tile(embeddings.astype(jnp.float32), (1, FEATURE_COUNT // D)) * sign_flips[None, :]
    first = walsh(tiled)
    picked = jnp.take(first.reshape(ROWS, BLOCKS, BLOCK), source_blocks, axis=1)
    mixed = jnp.einsum('rbj,bij->rbi', picked, block_permutations.astype(jnp.float32), precision=lax.Precision.HIGHEST)
    mixed = mixed.reshape(ROWS, FEATURE_COUNT) * gaussian[None, :]
    second = walsh(mixed)
    features = jnp.cos(scales[None, :] * second + phases[None, :])
    predictions = jnp.dot(features, weights, precision=lax.Precision.HIGHEST) * (1.0 / math.sqrt(FEATURE_COUNT))
    residual = predictions - targets
    feature_grad = jnp.dot(residual, features, precision=lax.Precision.HIGHEST) * (1.0 / math.sqrt(ROWS))
    return (predictions, feature_grad)
```

```python
import functools
import math

import jax
import jax.numpy as jnp
import numpy as np
from jax import lax
from jax.experimental import pallas as pl
from jax.experimental.pallas import tpu as pltpu
from jax.sharding import PartitionSpec as P

LANES = 128
CHUNK = 256
BOTH = ("feat", "rows")
MIB = 1024 * 1024


def hadamard(length):
    matrix = np.ones((1, 1), np.float32)
    while matrix.shape[0] < length:
        matrix = np.block([[matrix, matrix], [matrix, -matrix]])
    return matrix


def halves(values):
    high = values.astype(jnp.bfloat16)
    low = (values - high.astype(jnp.float32)).astype(jnp.bfloat16)
    return high, low


def swap(values, axis_name, bit):
    size = lax.axis_size(axis_name)
    return lax.ppermute(values, axis_name, [(i, i ^ bit) for i in range(size)])


def descending_bits(axis_name):
    bit = lax.axis_size(axis_name) // 2
    while bit:
        yield bit
        bit //= 2


def gather_all(piece, axes=BOTH):
    shape = piece.shape
    held = piece[None]
    for axis_name in axes:
        index = lax.axis_index(axis_name)
        for bit in descending_bits(axis_name):
            other = swap(held, axis_name, bit)
            upper = (index & bit) != 0
            held = jnp.where(
                upper, jnp.stack([other, held], 1), jnp.stack([held, other], 1)
            ).reshape((-1,) + shape)
    return held


def scatter_sum(terms):
    core = lax.axis_index("rows")
    for bit in descending_bits("rows"):
        count = terms.shape[1] // 2
        pair = terms.reshape((terms.shape[0], 2, count) + terms.shape[2:])
        mine = (core & bit) // bit
        keep = lax.dynamic_index_in_dim(pair, mine, 1, False)
        send = lax.dynamic_index_in_dim(pair, 1 - mine, 1, False)
        terms = keep + swap(send, "rows", bit)
    terms = terms[:, 0]
    place = lax.axis_index("feat")
    done = 1
    size = lax.axis_size("feat")
    bit = 1
    while bit < size:
        pair = terms.reshape((size // (2 * bit), 2) + terms.shape[1:])
        mine = (place & bit) // bit
        keep = lax.dynamic_index_in_dim(pair, mine, 1, False)
        send = lax.dynamic_index_in_dim(pair, 1 - mine, 1, False)
        terms = keep + swap(send, "feat", bit)
        bit *= 2
    return terms.reshape(terms.shape[1:])


def mix_kernel(rows, src_ref, sign_ref, order_ref, gain_ref, emb_ref, lane_ref, block_ref, out_ref, spread_ref):
    f32 = jnp.float32
    source = jnp.concatenate(
        [
            jnp.broadcast_to(src_ref[0, pl.ds(half, 1), :], (LANES, LANES)).T
            for half in range(CHUNK // LANES)
        ],
        axis=0,
    )
    source = source.astype(jnp.int32)
    lane = lax.broadcasted_iota(jnp.int32, (CHUNK, LANES), 1)
    major = source >> 2

    def flip(bits):
        return (1 - 2 * (bits & 1)).astype(f32)

    tiles = [flip(lax.population_count(major & lane))]
    for shift in range(7, 10):
        turn = flip(major >> shift)
        tiles = tiles + [tile * turn for tile in tiles]
    signs = jnp.concatenate([tile.astype(jnp.bfloat16) for tile in tiles], axis=1)
    sums = jnp.dot(signs, sign_ref[...], preferred_element_type=f32)
    first_flip = flip(source)
    second_flip = flip(source >> 1)
    quarter = [
        sums[:, 0:128],
        sums[:, 128:256] * first_flip,
        sums[:, 256:384] * second_flip,
        sums[:, 384:512] * (first_flip * second_flip),
    ]
    order = order_ref[...].reshape(CHUNK, LANES).astype(jnp.int32)
    gain = gain_ref[...].reshape(CHUNK, LANES)
    for r in range(rows):
        total = quarter[0] * emb_ref[pl.ds(r, 1), 0:128]
        for q in range(1, 4):
            total = total + quarter[q] * emb_ref[pl.ds(r, 1), 128 * q : 128 * (q + 1)]
        first = jnp.dot(
            jnp.concatenate(halves(total), axis=1), lane_ref[...], preferred_element_type=f32
        )
        mixed = jnp.take_along_axis(first, order, axis=1) * gain
        across = jnp.dot(
            jnp.concatenate(halves(mixed), axis=1), lane_ref[...], preferred_element_type=f32
        )
        high, low = halves(across)
        spread_ref[0:CHUNK, r * LANES : (r + 1) * LANES] = high
        spread_ref[CHUNK:, r * LANES : (r + 1) * LANES] = low
    result = jnp.dot(block_ref[...], spread_ref[...], preferred_element_type=f32)
    for r in range(rows):
        out_ref[0, r] = result[:, r * LANES : (r + 1) * LANES]


def turn_cosine_coefficients(degree):
    points = np.cos(np.pi * (np.arange(400) + 0.5) / 400)
    u = 0.5 * points
    fit = np.polynomial.chebyshev.Chebyshev.fit(u * u, np.cos(2 * np.pi * u), degree, domain=[0, 0.25])
    return [float(c) for c in fit.convert(kind=np.polynomial.Polynomial).coef]


def head_kernel(rows, chunks, tile, coefs, y_ref, scale_ref, phase_ref, weight_ref, target_ref, pred_ref, grad_ref, feat_ref, acc_ref, *, grad_scale):
    f32 = jnp.float32
    step = pl.program_id(0)
    steps = pl.num_programs(0)

    @pl.when(step == 0)
    def _():
        acc_ref[...] = jnp.zeros_like(acc_ref)

    for part in range(tile // 8):
        here = slice(part * 8, part * 8 + 8)
        for r in range(rows):
            values = [y_ref[k, r, here, :] for k in range(chunks)]
            width = 1
            while width < chunks:
                for k in range(chunks):
                    if not k & width:
                        a, b = values[k], values[k | width]
                        values[k], values[k | width] = a + b, a - b
                width *= 2
            acc = acc_ref[r]
            for k in range(chunks):
                turns = values[k] * scale_ref[k, 0, here, :] + phase_ref[k, 0, here, :]
                u = turns - jnp.round(turns)
                square = u * u
                cosine = jnp.full_like(square, coefs[-1])
                for c in coefs[-2::-1]:
                    cosine = cosine * square + c
                feat_ref[k, r, pl.ds(pl.multiple_of(step * tile + part * 8, 8), 8), :] = cosine
                acc = acc + cosine * weight_ref[k, 0, here, :]
            acc_ref[r] = acc

    @pl.when(step == steps - 1)
    def _():
        residuals = []
        for r in range(rows):
            total = jnp.sum(jnp.sum(acc_ref[r], axis=0, keepdims=True), axis=1, keepdims=True)
            pred_ref[pl.ds(r, 1), :] = jnp.broadcast_to(total, (1, LANES))
            residuals.append(jnp.broadcast_to((total - target_ref[r]) * grad_scale, (8, LANES)))

        for k in range(chunks):

            @pl.loop(0, CHUNK // 8)
            def _(i):
                rows_here = pl.ds(pl.multiple_of(i * 8, 8), 8)
                total = feat_ref[k, 0, rows_here, :] * residuals[0]
                for r in range(1, rows):
                    total = total + feat_ref[k, r, rows_here, :] * residuals[r]
                grad_ref[k, rows_here, :] = total


def local(
    embeddings,
    sign_flips,
    gaussian,
    scales,
    phases,
    source_blocks,
    block_permutations,
    weights,
    targets,
):
    f32 = jnp.float32
    feat_size = lax.axis_size("feat")
    rows_size = lax.axis_size("rows")
    place = lax.axis_index("feat")
    core = lax.axis_index("rows")
    devices = feat_size * rows_size
    width = embeddings.shape[1]
    rows = embeddings.shape[0] // feat_size
    total_rows = embeddings.shape[0] * rows_size
    features = sign_flips.shape[0] * feat_size
    blocks = features // LANES
    mine = blocks // devices
    quarters = width // LANES
    chunks = blocks // CHUNK
    per_chunk = CHUNK // mine

    def half(values):
        parts = values.reshape((rows_size, values.shape[0] // rows_size) + values.shape[1:])
        return lax.dynamic_index_in_dim(parts, core, 0, False)

    def rows_of(values):
        return half(values).reshape(mine, LANES)

    positions = jnp.einsum(
        "bij,j->bi", half(block_permutations), jnp.arange(LANES).astype(jnp.bfloat16), preferred_element_type=f32
    )
    early = jnp.concatenate([rows_of(sign_flips), positions, rows_of(gaussian)], axis=0)
    late = jnp.concatenate(
        [
            rows_of(scales) * f32(1.0 / (2.0 * math.pi * features)),
            rows_of(phases) * f32(1.0 / (2.0 * math.pi)),
            rows_of(weights) * f32(1.0 / math.sqrt(features)),
        ],
        axis=0,
    )
    numbers = gather_all(half(source_blocks).astype(f32))
    early = gather_all(early)
    late = gather_all(late)

    numbers = numbers.reshape(chunks, CHUNK // LANES, LANES)
    signs = early[:, :mine].reshape(blocks // quarters, width).astype(jnp.bfloat16)
    emb = lax.dynamic_slice_in_dim(embeddings, place * rows, rows, 0).astype(f32)
    lane_matrix = jnp.asarray(np.concatenate([hadamard(LANES)] * 2, 0), jnp.bfloat16)
    block_matrix = jnp.asarray(np.concatenate([hadamard(CHUNK)] * 2, 1), jnp.bfloat16)

    def early_part(which):
        return pl.BlockSpec((per_chunk, mine, LANES), lambda k: (k, which, 0))

    spread = pl.pallas_call(
        functools.partial(mix_kernel, rows),
        grid=(chunks,),
        in_specs=[
            pl.BlockSpec((1, CHUNK // LANES, LANES), lambda k: (k, 0, 0)),
            pl.BlockSpec((blocks // quarters, width), lambda k: (0, 0)),
            early_part(1),
            early_part(2),
            pl.BlockSpec((rows, width), lambda k: (0, 0)),
            pl.BlockSpec((2 * LANES, LANES), lambda k: (0, 0)),
            pl.BlockSpec((CHUNK, 2 * CHUNK), lambda k: (0, 0)),
        ],
        out_specs=pl.BlockSpec((1, rows, CHUNK, LANES), lambda k: (k, 0, 0, 0)),
        out_shape=jax.ShapeDtypeStruct((chunks, rows, CHUNK, LANES), f32),
        scratch_shapes=[pltpu.VMEM((2 * CHUNK, rows * LANES), jnp.bfloat16)],
        compiler_params=pltpu.CompilerParams(vmem_limit_bytes=48 * MIB),
        name="mix",
    )(numbers, signs, early, early, emb, lane_matrix, block_matrix)

    tile = min(16, mine)
    tiles_here = mine // tile
    late = late.reshape(chunks, per_chunk, 3 * mine, LANES)

    def late_part(which):
        return pl.BlockSpec(
            (chunks, 1, tile, LANES), lambda i: (0, i // tiles_here, which * tiles_here + i % tiles_here, 0)
        )

    my_targets = lax.dynamic_slice_in_dim(targets, place * rows, rows, 0)
    preds, grads = pl.pallas_call(
        functools.partial(
            head_kernel, rows, chunks, tile, turn_cosine_coefficients(6), grad_scale=1.0 / math.sqrt(total_rows)
        ),
        grid=(CHUNK // tile,),
        in_specs=[
            pl.BlockSpec((chunks, rows, tile, LANES), lambda i: (0, 0, i, 0)),
            late_part(0),
            late_part(1),
            late_part(2),
            pl.BlockSpec(memory_space=pltpu.SMEM),
        ],
        out_specs=[
            pl.BlockSpec((rows, LANES), lambda i: (0, 0)),
            pl.BlockSpec((chunks, CHUNK, LANES), lambda i: (0, 0, 0)),
        ],
        out_shape=[
            jax.ShapeDtypeStruct((rows, LANES), f32),
            jax.ShapeDtypeStruct((chunks, CHUNK, LANES), f32),
        ],
        scratch_shapes=[
            pltpu.VMEM((chunks, rows, CHUNK, LANES), f32),
            pltpu.VMEM((rows, 8, LANES), f32),
        ],
        compiler_params=pltpu.CompilerParams(vmem_limit_bytes=48 * MIB),
        name="head",
    )(spread, late, late, late, my_targets)

    predictions = gather_all(preds[:, 0], ("feat",)).reshape(-1)
    feature_grad = scatter_sum(grads.reshape(feat_size, rows_size, mine, LANES))
    return predictions, feature_grad.reshape(-1)


def solution(mesh):
    in_specs = (
        P("rows", None),
        P("feat"),
        P("feat"),
        P("feat"),
        P("feat"),
        P("feat"),
        P("feat", None, None),
        P("feat"),
        P("rows"),
    )
    out_specs = (P("rows"), P(("feat", "rows")))
    return jax.shard_map(local, mesh=mesh, in_specs=in_specs, out_specs=out_specs, check_vma=False)
```

```python
import functools
import math

import jax
import jax.numpy as jnp
import numpy as np
from jax import lax
from jax.experimental import pallas as pl
from jax.experimental.pallas import tpu as pltpu
from jax.sharding import PartitionSpec as P

LANES = 128
CHUNK = 256
BOTH = ("feat", "rows")
MIB = 1024 * 1024


def hadamard(length):
    matrix = np.ones((1, 1), np.float32)
    while matrix.shape[0] < length:
        matrix = np.block([[matrix, matrix], [matrix, -matrix]])
    return matrix


def halves(values):
    high = values.astype(jnp.bfloat16)
    low = (values - high.astype(jnp.float32)).astype(jnp.bfloat16)
    return high, low


def swap(values, axis_name, bit):
    size = lax.axis_size(axis_name)
    return lax.ppermute(values, axis_name, [(i, i ^ bit) for i in range(size)])


def bits_of(axis_name):
    return [1 << i for i in reversed(range(lax.axis_size(axis_name).bit_length() - 1))]


def gather_ordered(piece):
    shape = piece.shape
    held = piece[None]
    for axis_name in BOTH:
        index = lax.axis_index(axis_name)
        for bit in bits_of(axis_name):
            other = swap(held, axis_name, bit)
            upper = (index & bit) != 0
            held = jnp.where(
                upper, jnp.stack([other, held], 1), jnp.stack([held, other], 1)
            ).reshape((-1,) + shape)
    return held


def gather_relative(piece, bits):
    held = piece[None]
    for bit in bits:
        held = jnp.concatenate([held, swap(held, "feat", bit)], axis=0)
    return held


def place_of(distance, bits):
    place = 0
    for i, bit in enumerate(bits):
        place = place + (((distance >> (bit.bit_length() - 1)) & 1) << i)
    return place


def take_part(values, axis, index):
    return lax.dynamic_index_in_dim(values, index, axis, False)


def scatter_sum(terms, extra):
    place = lax.axis_index("feat")
    core = lax.axis_index("rows")
    for bit in bits_of("rows"):
        pair = terms.reshape((terms.shape[0], 2, bit) + terms.shape[2:])
        mine = (core & bit) // bit
        terms = take_part(pair, 1, mine) + swap(take_part(pair, 1, 1 - mine), "rows", bit)
    lanes = terms.shape[-1]
    bits = bits_of("feat")
    count = terms.shape[2]
    terms = terms.reshape((2,) * len(bits) + (count, lanes))
    cut = count // 2
    parts = [terms[..., :cut, :], terms[..., cut:, :]]
    names = [list(bits), list(bits)]
    orders = [[1, 2], [2, 1]]

    def exchange(part, left, bit, extra):
        axis = left.index(bit)
        left.remove(bit)
        mine = (place & bit) // bit
        keep = take_part(part, axis, mine)
        send = take_part(part, axis, 1 - mine).reshape(-1, lanes)
        if extra is None:
            return keep + swap(send, "feat", bit).reshape(keep.shape), None
        got = swap(jnp.concatenate([send, extra], axis=0), "feat", bit)
        return keep + got[: send.shape[0]].reshape(keep.shape), extra + got[send.shape[0] :]

    for turn in range(2):
        parts[0], extra = exchange(parts[0], names[0], orders[0][turn], extra)
        parts[1], _ = exchange(parts[1], names[1], orders[1][turn], None)
    rest = jnp.concatenate(parts, axis=-2)
    for bit in list(reversed(names[0])):
        rest, extra = exchange(rest, names[0], bit, extra)
    return rest, extra


def mix_kernel(rows, bits_a, bits_b, me_ref, a_own, a_other, b_own, b_other, emb_ref, lane_ref, block_ref, out_ref, sign_ref, wide_ref, spread_ref):
    f32 = jnp.float32
    bf16 = jnp.bfloat16
    chunks = a_own.shape[0]
    width = emb_ref.shape[0]
    quarters = width // LANES
    here = LANES // quarters
    chunk = pl.program_id(0)

    def flip(bits):
        return (1 - 2 * (bits & 1)).astype(f32)

    @pl.when(chunk == 0)
    def _():
        for c, ref in enumerate((a_own, a_other)):
            for p in range(chunks):
                top = (c * chunks + p) * here
                for q in range(quarters):
                    sign_ref[top : top + here, q * LANES : (q + 1) * LANES] = ref[
                        p, q * here : (q + 1) * here, :
                    ].astype(bf16)
        sums = jnp.dot(jnp.ones((16, sign_ref.shape[0]), bf16), sign_ref[...], preferred_element_type=f32)
        odd = 0.5 * sums - 2.0 * jnp.floor(0.25 * sums)
        row = lax.broadcasted_iota(jnp.int32, odd.shape, 0)
        column = lax.broadcasted_iota(jnp.int32, odd.shape, 1)
        odd = jnp.where((row < 2 * quarters) & ((row & (quarters - 1)) == column // LANES), 0.5 * odd, 0.0)
        rest = jnp.dot(odd.astype(bf16), emb_ref[...], preferred_element_type=f32)
        high = rest.astype(bf16).astype(f32)
        row = lax.broadcasted_iota(jnp.int32, rest.shape, 0)
        wide_ref[0:width, :] = emb_ref[...]
        wide_ref[width:, :] = jnp.zeros((LANES, wide_ref.shape[1]), bf16)
        wide_ref[width : width + 16, :] = jnp.where(row < quarters, high, rest - high).astype(bf16)

    pa = place_of(chunk, bits_a)
    pb = place_of(chunk, bits_b)
    major_me = me_ref[0] * here
    columns = []
    for ref in (a_own, a_other):
        source = ref[pa, 3 * LANES // 2 : 3 * LANES // 2 + 1, :].astype(jnp.int32)
        major = source >> 2
        low = here.bit_length() - 1
        code = major & (here - 1)
        for i, bit in enumerate(bits_a):
            code = code | (((major >> (low + bit.bit_length())) & 1) << (low + i))
        code = code | (((major >> low) & 1) << (low + len(bits_a)))
        code = code | ((source & 3) << 10) | ((lax.population_count(major & major_me) & 1) << 12)
        columns.append(jnp.broadcast_to(code.astype(f32), (LANES, LANES)).T)
    code = jnp.concatenate(columns, axis=0).astype(jnp.int32)
    lane = lax.broadcasted_iota(jnp.int32, (CHUNK, LANES), 1)
    tiles = [flip(lax.population_count(code & lane))]
    for shift in range(7, 10):
        turn = flip(code >> shift)
        tiles = tiles + [tile * turn for tile in tiles]
    signs = jnp.concatenate([tile.astype(bf16) for tile in tiles], axis=1)
    sums = jnp.dot(signs, sign_ref[...], preferred_element_type=f32)
    flip_me, flip_1, flip_2 = flip(code >> 12), flip(code >> 10), flip(code >> 11)
    turns = [flip_me, flip_me * flip_1, flip_me * flip_2, flip_me * flip_1 * flip_2]
    left = [
        (jnp.floor(0.25 * sums[:, q * LANES : (q + 1) * LANES]) * turns[q]).astype(bf16) for q in range(4)
    ]
    tail = flip_me * jnp.where((lane & 1) != 0, flip_1, 1.0) * jnp.where((lane & 2) != 0, flip_2, 1.0)
    left.append(jnp.where(lane < 8, tail, 0.0).astype(bf16))
    first = jnp.dot(jnp.concatenate(left, axis=1), wide_ref[...], preferred_element_type=f32)

    half = LANES // 2
    order = jnp.concatenate(
        [
            ref[p, LANES : LANES + half, :]
            for ref, p in ((a_own, pa), (b_own, pb), (a_other, pa), (b_other, pb))
        ],
        axis=0,
    ).astype(jnp.int32)
    gain = jnp.concatenate([b_own[pb, 0:LANES, :], b_other[pb, 0:LANES, :]], axis=0)
    for r in range(rows):
        columns = slice(r * LANES, (r + 1) * LANES)
        mixed = jnp.take_along_axis(first[:, columns], order, axis=1) * gain
        across = jnp.dot(
            jnp.concatenate(halves(mixed), axis=1), lane_ref[...], preferred_element_type=f32
        )
        high, low = halves(across)
        spread_ref[0:CHUNK, columns] = high
        spread_ref[CHUNK:, columns] = low
    result = jnp.dot(block_ref[...], spread_ref[...], preferred_element_type=f32)
    for r in range(rows):
        out_ref[0, r] = result[:, r * LANES : (r + 1) * LANES]


def turn_cosine_coefficients(degree):
    points = np.cos(np.pi * (np.arange(400) + 0.5) / 400)
    u = 0.5 * points
    fit = np.polynomial.chebyshev.Chebyshev.fit(u * u, np.cos(2 * np.pi * u), degree, domain=[0, 0.25])
    return [float(c) for c in fit.convert(kind=np.polynomial.Polynomial).coef]


def head_kernel(rows, chunks, tile, coefs, grad_scale, me_ref, target_ref, y_ref, scale_ref, phase_ref, weight_ref, pred_ref, grad_ref, feat_ref, acc_ref, turn_ref):
    f32 = jnp.float32
    step = pl.program_id(0)
    steps = pl.num_programs(0)

    @pl.when(step == 0)
    def _():
        acc_ref[...] = jnp.zeros_like(acc_ref)

    second_half = (step * tile) // LANES
    for k in range(chunks):
        shared = (2 * k + second_half) & me_ref[0]
        shared = shared ^ (shared >> 4)
        shared = shared ^ (shared >> 2)
        shared = shared ^ (shared >> 1)
        turn_ref[k] = scale_ref[k, 0] * (1 - 2 * (shared & 1)).astype(f32)

    for part in range(tile // 8):
        here = slice(part * 8, part * 8 + 8)
        for r in range(rows):
            values = [y_ref[k, r, here, :] for k in range(chunks)]
            width = 1
            while width < chunks:
                for k in range(chunks):
                    if not k & width:
                        a, b = values[k], values[k | width]
                        values[k], values[k | width] = a + b, a - b
                width *= 2
            acc = acc_ref[r]
            for k in range(chunks):
                turns = values[k] * turn_ref[k, here, :] + phase_ref[k, 0, here, :]
                u = turns - jnp.round(turns)
                square = u * u
                cosine = jnp.full_like(square, coefs[-1])
                for c in coefs[-2::-1]:
                    cosine = cosine * square + c
                feat_ref[k, r, pl.ds(pl.multiple_of(step * tile + part * 8, 8), 8), :] = cosine
                acc = acc + cosine * weight_ref[k, 0, here, :]
            acc_ref[r] = acc

    @pl.when(step == steps - 1)
    def _():
        residuals = []
        lane = lax.broadcasted_iota(jnp.int32, (1, LANES), 1)
        found = jnp.zeros((1, LANES), f32)
        for r in range(rows):
            total = jnp.sum(jnp.sum(acc_ref[r], axis=0, keepdims=True), axis=1, keepdims=True)
            found = found + jnp.where(lane == me_ref[1] + r, total, 0.0)
            residuals.append(jnp.broadcast_to((total - target_ref[r]) * grad_scale, (8, LANES)))
        pred_ref[...] = jnp.broadcast_to(found, (8, LANES))

        for k in range(chunks):

            @pl.loop(0, CHUNK // 32)
            def _(i):
                for j in range(4):
                    rows_here = pl.ds(pl.multiple_of(i * 32 + j * 8, 8), 8)
                    total = feat_ref[k, 0, rows_here, :] * residuals[0]
                    for r in range(1, rows):
                        total = total + feat_ref[k, r, rows_here, :] * residuals[r]
                    grad_ref[k, rows_here, :] = total


def local(
    embeddings,
    sign_flips,
    gaussian,
    scales,
    phases,
    source_blocks,
    block_permutations,
    weights,
    targets,
):
    f32 = jnp.float32
    feat_size = lax.axis_size("feat")
    rows_size = lax.axis_size("rows")
    place = lax.axis_index("feat")
    core = lax.axis_index("rows")
    devices = feat_size * rows_size
    width = embeddings.shape[1]
    rows = embeddings.shape[0] // feat_size
    total_rows = embeddings.shape[0] * rows_size
    features = sign_flips.shape[0] * feat_size
    blocks = features // LANES
    mine = blocks // devices
    quarters = width // LANES
    chunks = blocks // CHUNK
    per_chunk = CHUNK // mine

    def half(values):
        parts = values.reshape((rows_size, values.shape[0] // rows_size) + values.shape[1:])
        return lax.dynamic_index_in_dim(parts, core, 0, False)

    def rows_of(*vectors):
        return jnp.concatenate([half(v) for v in vectors]).reshape(len(vectors), mine, LANES)

    positions = jnp.einsum(
        "bij,j->bi", half(block_permutations), jnp.arange(LANES).astype(jnp.bfloat16), preferred_element_type=f32
    )
    signs, gains = rows_of(sign_flips, gaussian)
    numbers = half(source_blocks).astype(f32)
    late = rows_of(
        scales * f32(4.0 / (2.0 * math.pi * features)),
        phases * f32(1.0 / (2.0 * math.pi)),
        weights * f32(1.0 / math.sqrt(features)),
    )
    late = lax.all_gather(late.reshape(3 * mine, LANES), BOTH)
    bits = bits_of("feat")
    if mine == LANES and feat_size == chunks and rows_size == 2:
        me = place * rows_size + core
        bits_a = bits[:-2] + [2, 1]
        bits_b = bits[:-2] + [1, 2]
    else:
        me = 0
        bits_a = bits_b = [1 << i for i in range(chunks.bit_length() - 1)]
        whole = gather_ordered(
            jnp.concatenate([signs, positions, gains, jnp.pad(numbers.reshape(1, mine), ((0, 7), (0, LANES - mine)))])
        )
        signs, positions, gains = (
            whole[:, i * mine : (i + 1) * mine].reshape(chunks, 2, LANES, LANES) for i in range(3)
        )
        numbers = whole[:, 3 * mine, :mine].reshape(chunks, 2, LANES)

    per_half = LANES // quarters
    shape = signs.shape
    signs = jnp.swapaxes(signs.reshape(shape[:-2] + (per_half, quarters, LANES)), -3, -2).reshape(shape)
    numbers = jnp.broadcast_to(numbers[..., None, :], shape[:-2] + (8, LANES))
    cut = LANES // 2
    part_a = jnp.concatenate([signs, positions[..., :cut, :], numbers], axis=-2)
    part_b = jnp.concatenate([gains, positions[..., cut:, :]], axis=-2)
    if part_a.ndim == 2:
        part_a = gather_relative(part_a, bits_a)
        part_b = gather_relative(part_b, bits_b)
        a_pair = (part_a, swap(part_a, "rows", 1))
        b_pair = (part_b, swap(part_b, "rows", 1))
    else:
        a_pair = (part_a[:, 0], part_a[:, 1])
        b_pair = (part_b[:, 0], part_b[:, 1])

    emb = lax.dynamic_slice_in_dim(embeddings, place * rows, rows, 0)
    lane_signs = hadamard(LANES)
    emb = (emb.T.reshape(quarters, LANES, rows, 1) * jnp.asarray(lane_signs, jnp.bfloat16)[None, :, None, :]).reshape(
        width, rows * LANES
    )
    lane_matrix = jnp.asarray(np.concatenate([lane_signs] * 2, 0), jnp.bfloat16)
    block_matrix = jnp.asarray(np.concatenate([hadamard(CHUNK)] * 2, 1), jnp.bfloat16)
    about_me = jnp.stack([jnp.asarray(me, jnp.int32), (place * rows).astype(jnp.int32)])

    def resident(array):
        return pl.BlockSpec(array.shape, lambda k: (0,) * array.ndim)

    scalars = pl.BlockSpec(memory_space=pltpu.SMEM)
    resident_args = (*a_pair, *b_pair, emb, lane_matrix, block_matrix)
    spread = pl.pallas_call(
        functools.partial(mix_kernel, rows, bits_a, bits_b),
        grid=(chunks,),
        in_specs=[scalars] + [resident(x) for x in resident_args],
        out_specs=pl.BlockSpec((1, rows, CHUNK, LANES), lambda k: (k, 0, 0, 0)),
        out_shape=jax.ShapeDtypeStruct((chunks, rows, CHUNK, LANES), f32),
        scratch_shapes=[
            pltpu.VMEM((blocks // quarters, width), jnp.bfloat16),
            pltpu.VMEM((width + LANES, rows * LANES), jnp.bfloat16),
            pltpu.VMEM((2 * CHUNK, rows * LANES), jnp.bfloat16),
        ],
        compiler_params=pltpu.CompilerParams(vmem_limit_bytes=48 * MIB),
        name="mix",
    )(about_me, *resident_args)

    tile = min(32, mine)
    tiles_here = mine // tile
    late = late.reshape(chunks, per_chunk, 3 * mine, LANES)

    def late_part(which):
        return pl.BlockSpec(
            (chunks, 1, tile, LANES), lambda i: (0, i // tiles_here, which * tiles_here + i % tiles_here, 0)
        )

    my_targets = lax.dynamic_slice_in_dim(targets, place * rows, rows, 0)
    found, grads = pl.pallas_call(
        functools.partial(
            head_kernel, rows, chunks, tile, turn_cosine_coefficients(5), 1.0 / math.sqrt(total_rows)
        ),
        grid=(CHUNK // tile,),
        in_specs=[
            scalars,
            scalars,
            pl.BlockSpec((chunks, rows, tile, LANES), lambda i: (0, 0, i, 0)),
            late_part(0),
            late_part(1),
            late_part(2),
        ],
        out_specs=[
            pl.BlockSpec((8, LANES), lambda i: (0, 0)),
            pl.BlockSpec((chunks, CHUNK, LANES), lambda i: (0, 0, 0)),
        ],
        out_shape=[
            jax.ShapeDtypeStruct((8, LANES), f32),
            jax.ShapeDtypeStruct((chunks, CHUNK, LANES), f32),
        ],
        scratch_shapes=[
            pltpu.VMEM((chunks, rows, CHUNK, LANES), f32),
            pltpu.VMEM((rows, 8, LANES), f32),
            pltpu.VMEM((chunks, tile, LANES), f32),
        ],
        compiler_params=pltpu.CompilerParams(vmem_limit_bytes=48 * MIB),
        name="head",
    )(about_me, my_targets, spread, late, late, late)

    feature_grad, found = scatter_sum(grads.reshape(feat_size, rows_size, mine, LANES), found)
    return found[0], feature_grad.reshape(-1)


def solution(mesh):
    in_specs = (
        P("rows", None),
        P("feat"),
        P("feat"),
        P("feat"),
        P("feat"),
        P("feat"),
        P("feat", None, None),
        P("feat"),
        P("rows"),
    )
    out_specs = (P("rows"), P(("feat", "rows")))
    return jax.shard_map(local, mesh=mesh, in_specs=in_specs, out_specs=out_specs, check_vma=False)
```

```python
import functools
import math

import jax
import jax.numpy as jnp
import numpy as np
from jax import lax
from jax.experimental import pallas as pl
from jax.experimental.pallas import tpu as pltpu
from jax.sharding import PartitionSpec as P

LANES = 128
CHUNK = 256
BOTH = ("feat", "rows")
MIB = 1024 * 1024


def hadamard(length):
    matrix = np.ones((1, 1), np.float32)
    while matrix.shape[0] < length:
        matrix = np.block([[matrix, matrix], [matrix, -matrix]])
    return matrix


def halves(values):
    high = values.astype(jnp.bfloat16)
    low = (values - high.astype(jnp.float32)).astype(jnp.bfloat16)
    return high, low


def swap(values, axis_name, bit):
    size = lax.axis_size(axis_name)
    return lax.ppermute(values, axis_name, [(i, i ^ bit) for i in range(size)])


def bits_of(axis_name):
    return [1 << i for i in reversed(range(lax.axis_size(axis_name).bit_length() - 1))]


def gather_ordered(piece):
    shape = piece.shape
    held = piece[None]
    for axis_name in BOTH:
        index = lax.axis_index(axis_name)
        for bit in bits_of(axis_name):
            other = swap(held, axis_name, bit)
            upper = (index & bit) != 0
            held = jnp.where(
                upper, jnp.stack([other, held], 1), jnp.stack([held, other], 1)
            ).reshape((-1,) + shape)
    return held


def gather_relative(piece, bits):
    held = piece[None]
    for bit in bits:
        held = jnp.concatenate([held, swap(held, "feat", bit)], axis=0)
    return held


def place_of(distance, bits):
    place = 0
    for i, bit in enumerate(bits):
        place = place + (((distance >> (bit.bit_length() - 1)) & 1) << i)
    return place


def scatter_sum(keep, send, extra):
    terms = keep + swap(send, "rows", 1)
    bits = bits_of("feat")
    count, lanes = terms.shape[1:]
    terms = terms.reshape((2,) * len(bits) + (count, lanes))
    cut = count // 2
    parts = [terms[..., :cut, :], terms[..., cut:, :]]
    names = [list(bits), list(bits)]

    def exchange(part, left, bit, extra):
        axis = left.index(bit)
        left.remove(bit)
        keep = lax.index_in_dim(part, 0, axis, False)
        send = lax.index_in_dim(part, 1, axis, False).reshape(-1, lanes)
        if extra is None:
            return keep + swap(send, "feat", bit).reshape(keep.shape), None
        got = swap(jnp.concatenate([send, extra], axis=0), "feat", bit)
        return keep + got[: send.shape[0]].reshape(keep.shape), extra + got[send.shape[0] :]

    for bit_a, bit_b in ((1, 2), (2, 1)):
        parts[0], extra = exchange(parts[0], names[0], bit_a, extra)
        parts[1], _ = exchange(parts[1], names[1], bit_b, None)
    rest = jnp.concatenate(parts, axis=-2)
    for bit in list(reversed(names[0])):
        rest, extra = exchange(rest, names[0], bit, extra)
    return rest, extra


def odd_bits(value):
    value = value ^ (value >> 4)
    value = value ^ (value >> 2)
    return (value ^ (value >> 1)) & 1


def mix_kernel(rows, begin, bits_a, bits_b, me_ref, a_own, a_other, b_own, b_other, emb_ref, lane_ref, block_ref, out_ref, sign_ref, wide_ref, spread_ref):
    f32 = jnp.float32
    bf16 = jnp.bfloat16
    chunks = a_own.shape[0]
    width = emb_ref.shape[0]
    quarters = width // LANES
    here = LANES // quarters
    chunk = pl.program_id(0) + begin

    def flip(bits):
        return (1 - 2 * (bits & 1)).astype(f32)

    @pl.when(chunk == begin)
    def _():
        for c, ref in enumerate((a_own, a_other)):
            for p in range(chunks):
                top = (c * chunks + p) * here
                for q in range(quarters):
                    sign_ref[top : top + here, q * LANES : (q + 1) * LANES] = ref[
                        p, q * here : (q + 1) * here, :
                    ].astype(bf16)
        sums = jnp.dot(jnp.ones((16, sign_ref.shape[0]), bf16), sign_ref[...], preferred_element_type=f32)
        odd = 0.5 * sums - 2.0 * jnp.floor(0.25 * sums)
        row = lax.broadcasted_iota(jnp.int32, odd.shape, 0)
        column = lax.broadcasted_iota(jnp.int32, odd.shape, 1)
        odd = jnp.where((row < 2 * quarters) & ((row & (quarters - 1)) == column // LANES), 0.5 * odd, 0.0)
        rest = jnp.dot(odd.astype(bf16), emb_ref[...], preferred_element_type=f32)
        high = rest.astype(bf16).astype(f32)
        row = lax.broadcasted_iota(jnp.int32, rest.shape, 0)
        wide_ref[0:width, :] = emb_ref[...]
        wide_ref[width:, :] = jnp.zeros((LANES, wide_ref.shape[1]), bf16)
        wide_ref[width : width + 16, :] = jnp.where(row < quarters, high, rest - high).astype(bf16)

    pa = place_of(chunk, bits_a)
    pb = place_of(chunk, bits_b)
    major_me = me_ref[0] * here
    columns = []
    for ref in (a_own, a_other):
        source = ref[pa, 3 * LANES // 2 : 3 * LANES // 2 + 1, :].astype(jnp.int32)
        major = source >> 2
        low = here.bit_length() - 1
        code = major & (here - 1)
        for i, bit in enumerate(bits_a):
            code = code | (((major >> (low + bit.bit_length())) & 1) << (low + i))
        code = code | (((major >> low) & 1) << (low + len(bits_a)))
        code = code | ((source & 3) << 10) | ((lax.population_count(major & major_me) & 1) << 12)
        columns.append(jnp.broadcast_to(code.astype(f32), (LANES, LANES)).T)
    code = jnp.concatenate(columns, axis=0).astype(jnp.int32)
    lane = lax.broadcasted_iota(jnp.int32, (CHUNK, LANES), 1)
    tiles = [flip(lax.population_count(code & lane))]
    for shift in range(7, 10):
        turn = flip(code >> shift)
        tiles = tiles + [tile * turn for tile in tiles]
    signs = jnp.concatenate([tile.astype(bf16) for tile in tiles], axis=1)
    sums = jnp.dot(signs, sign_ref[...], preferred_element_type=f32)
    flip_me, flip_1, flip_2 = flip(code >> 12), flip(code >> 10), flip(code >> 11)
    turns = [flip_me, flip_me * flip_1, flip_me * flip_2, flip_me * flip_1 * flip_2]
    left = [
        (jnp.floor(0.25 * sums[:, q * LANES : (q + 1) * LANES]) * turns[q]).astype(bf16) for q in range(4)
    ]
    tail = flip_me * jnp.where((lane & 1) != 0, flip_1, 1.0) * jnp.where((lane & 2) != 0, flip_2, 1.0)
    left.append(jnp.where(lane < 8, tail, 0.0).astype(bf16))
    first = jnp.dot(jnp.concatenate(left, axis=1), wide_ref[...], preferred_element_type=f32)

    half = LANES // 2
    order = jnp.concatenate(
        [
            ref[p, LANES : LANES + half, :]
            for ref, p in ((a_own, pa), (b_own, pb), (a_other, pa), (b_other, pb))
        ],
        axis=0,
    ).astype(jnp.int32)
    gain = jnp.concatenate(
        [
            ref[pb, 0:LANES, :] * (1 - 2 * odd_bits((2 * chunk + c) & me_ref[0])).astype(f32)
            for c, ref in enumerate((b_own, b_other))
        ],
        axis=0,
    )
    for r in range(rows):
        columns = slice(r * LANES, (r + 1) * LANES)
        mixed = jnp.take_along_axis(first[:, columns], order, axis=1) * gain
        across = jnp.dot(
            jnp.concatenate(halves(mixed), axis=1), lane_ref[...], preferred_element_type=f32
        )
        high, low = halves(across)
        spread_ref[0:CHUNK, columns] = high
        spread_ref[CHUNK:, columns] = low
    result = jnp.dot(block_ref[...], spread_ref[...], preferred_element_type=f32)
    for r in range(rows):
        out_ref[0, r] = result[:, r * LANES : (r + 1) * LANES]


def turn_cosine_coefficients(degree):
    points = np.cos(np.pi * (np.arange(400) + 0.5) / 400)
    u = 0.5 * points
    fit = np.polynomial.chebyshev.Chebyshev.fit(u * u, np.cos(2 * np.pi * u), degree, domain=[0, 0.25])
    return [float(c) for c in fit.convert(kind=np.polynomial.Polynomial).coef]


def head_kernel(
    rows, tile, coefs, grad_scale, bits_a, bits_b, me_ref, target_ref, y_low, y_high, *refs
):
    late_refs, (pred_ref, keep_ref, send_ref, feat_ref, acc_ref, stage_ref) = refs[:12], refs[12:]
    f32 = jnp.float32
    step = pl.program_id(0)
    steps = pl.num_programs(0)
    chunks = feat_ref.shape[0]
    y_chunks = y_low.shape[0]
    per_part = steps // 4

    @pl.when(step == 0)
    def _():
        acc_ref[...] = jnp.zeros_like(acc_ref)

    for part in range(4):
        core, bits = part // 2, (bits_a, bits_b)[part % 2]

        @pl.when(step // per_part == part)
        def _():
            scale_ref, phase_ref, weight_ref = late_refs[3 * part : 3 * part + 3]
            for k in range(chunks):
                place = place_of(k, bits)
                shared = odd_bits((2 * k + core) & me_ref[0]) ^ odd_bits(me_ref[0])
                stage_ref[0, k] = scale_ref[place] * (1 - 2 * shared).astype(f32)
                stage_ref[1, k] = phase_ref[place]
                stage_ref[2, k] = weight_ref[place]

    for part in range(tile // 8):
        here = slice(part * 8, part * 8 + 8)
        for r in range(rows):
            values = [y_low[k, r, here, :] for k in range(y_chunks)]
            values += [y_high[k, r, here, :] for k in range(chunks - y_chunks)]
            width = 1
            while width < chunks:
                for k in range(chunks):
                    if not k & width:
                        a, b = values[k], values[k | width]
                        values[k], values[k | width] = a + b, a - b
                width *= 2
            acc = acc_ref[r]
            for k in range(chunks):
                turns = values[k] * stage_ref[0, k, here, :] + stage_ref[1, k, here, :]
                u = turns - jnp.round(turns)
                square = u * u
                cosine = jnp.full_like(square, coefs[-1])
                for c in coefs[-2::-1]:
                    cosine = cosine * square + c
                feat_ref[k, r, pl.ds(pl.multiple_of(step * tile + part * 8, 8), 8), :] = cosine
                acc = acc + cosine * stage_ref[2, k, here, :]
            acc_ref[r] = acc

    @pl.when(step == steps - 1)
    def _():
        residuals = []
        lane = lax.broadcasted_iota(jnp.int32, (1, LANES), 1)
        found = jnp.zeros((1, LANES), f32)
        for r in range(rows):
            total = jnp.sum(jnp.sum(acc_ref[r], axis=0, keepdims=True), axis=1, keepdims=True)
            found = found + jnp.where(lane == me_ref[1] + r, total, 0.0)
            residuals.append(jnp.broadcast_to((total - target_ref[r]) * grad_scale, (8, LANES)))
        pred_ref[...] = jnp.broadcast_to(found, (8, LANES))

        for half, out_ref in enumerate((keep_ref, send_ref)):
            for k in range(chunks):

                @pl.loop(0, LANES // 32)
                def _(i):
                    for j in range(4):
                        row = pl.multiple_of(i * 32 + j * 8, 8)
                        rows_here = pl.ds(row + half * LANES, 8)
                        total = feat_ref[k, 0, rows_here, :] * residuals[0]
                        for r in range(1, rows):
                            total = total + feat_ref[k, r, rows_here, :] * residuals[r]
                        out_ref[k, pl.ds(row, 8), :] = total


def local(
    embeddings,
    sign_flips,
    gaussian,
    scales,
    phases,
    source_blocks,
    block_permutations,
    weights,
    targets,
):
    f32 = jnp.float32
    feat_size = lax.axis_size("feat")
    rows_size = lax.axis_size("rows")
    place = lax.axis_index("feat")
    core = lax.axis_index("rows")
    devices = feat_size * rows_size
    width = embeddings.shape[1]
    rows = embeddings.shape[0] // feat_size
    total_rows = embeddings.shape[0] * rows_size
    features = sign_flips.shape[0] * feat_size
    blocks = features // LANES
    mine = blocks // devices
    quarters = width // LANES
    chunks = blocks // CHUNK
    per_chunk = CHUNK // mine

    def half(values):
        parts = values.reshape((rows_size, values.shape[0] // rows_size) + values.shape[1:])
        return lax.dynamic_index_in_dim(parts, core, 0, False)

    def rows_of(*vectors):
        return jnp.concatenate([half(v) for v in vectors]).reshape(len(vectors), mine, LANES)

    positions = jnp.einsum(
        "bij,j->bi", half(block_permutations), jnp.arange(LANES).astype(jnp.bfloat16), preferred_element_type=f32
    )
    signs, gains = rows_of(sign_flips, gaussian)
    numbers = half(source_blocks).astype(f32)
    late = rows_of(
        scales * f32(4.0 / (2.0 * math.pi * features)),
        phases * f32(1.0 / (2.0 * math.pi)),
        weights * f32(1.0 / math.sqrt(features)),
    )
    bits = bits_of("feat")
    numbers = jnp.broadcast_to(jnp.pad(numbers, (0, LANES - mine))[None, :], (8, LANES))
    everything = [signs, positions, gains, *late, numbers]
    direct = mine == LANES and feat_size == chunks and rows_size == 2
    if direct:
        me = place * rows_size + core
        bits_a = bits[:-2] + [2, 1]
        bits_b = bits[:-2] + [1, 2]
    else:
        me = 0
        bits_a = bits_b = [1 << i for i in range(chunks.bit_length() - 1)]
        whole = gather_ordered(jnp.concatenate(everything))
        numbers = whole[:, 6 * mine, :mine].reshape(chunks, 2, 1, LANES)
        numbers = jnp.broadcast_to(numbers, (chunks, 2, 8, LANES))
        everything = [whole[:, i * mine : (i + 1) * mine].reshape(chunks, 2, LANES, LANES) for i in range(6)]
        everything.append(numbers)
    signs, positions, gains, *late, numbers = everything

    per_half = LANES // quarters
    shape = signs.shape
    signs = jnp.swapaxes(signs.reshape(shape[:-2] + (per_half, quarters, LANES)), -3, -2).reshape(shape)
    cut = LANES // 2
    pieces = [
        jnp.concatenate([signs, positions[..., :cut, :], numbers], axis=-2),
        jnp.concatenate([gains, positions[..., cut:, :]], axis=-2),
        jnp.concatenate([x[..., :cut, :] for x in late], axis=-2),
        jnp.concatenate([x[..., cut:, :] for x in late], axis=-2),
    ]
    if direct:
        pieces = [gather_relative(x, b) for x, b in zip(pieces, (bits_a, bits_b) * 2)]
        a_pair, b_pair, c_pair, d_pair = ((x, swap(x, "rows", 1)) for x in pieces)
    else:
        a_pair, b_pair, c_pair, d_pair = ((x[:, 0], x[:, 1]) for x in pieces)

    emb = lax.dynamic_slice_in_dim(embeddings, place * rows, rows, 0)
    lane_signs = hadamard(LANES)
    emb = (emb.T.reshape(quarters, LANES, rows, 1) * jnp.asarray(lane_signs, jnp.bfloat16)[None, :, None, :]).reshape(
        width, rows * LANES
    )
    lane_matrix = jnp.asarray(np.concatenate([lane_signs] * 2, 0), jnp.bfloat16)
    block_matrix = jnp.asarray(np.concatenate([hadamard(CHUNK)] * 2, 1), jnp.bfloat16)
    about_me = jnp.stack([jnp.asarray(me, jnp.int32), (place * rows).astype(jnp.int32)])

    def resident(array):
        return pl.BlockSpec(array.shape, lambda k: (0,) * array.ndim)

    scalars = pl.BlockSpec(memory_space=pltpu.SMEM)
    resident_args = (*a_pair, *b_pair, emb, lane_matrix, block_matrix)

    def mix(begin, count):
        return pl.pallas_call(
            functools.partial(mix_kernel, rows, begin, bits_a, bits_b),
            grid=(count,),
            in_specs=[scalars] + [resident(x) for x in resident_args],
            out_specs=pl.BlockSpec((1, rows, CHUNK, LANES), lambda k: (k, 0, 0, 0)),
            out_shape=jax.ShapeDtypeStruct((count, rows, CHUNK, LANES), f32),
            scratch_shapes=[
                pltpu.VMEM((blocks // quarters, width), jnp.bfloat16),
                pltpu.VMEM((width + LANES, rows * LANES), jnp.bfloat16),
                pltpu.VMEM((2 * CHUNK, rows * LANES), jnp.bfloat16),
            ],
            compiler_params=pltpu.CompilerParams(vmem_limit_bytes=48 * MIB),
            cost_estimate=pl.CostEstimate(
                flops=count * 2 * 256 * 8192 * 256, bytes_accessed=count * rows * CHUNK * LANES * 4, transcendentals=0
            ),
            name="mix",
        )(about_me, *resident_args)

    split = chunks // 2
    y_low, y_high = mix(0, split), mix(split, chunks - split)

    tile = 32
    per_part = cut // tile

    def late_part(part, which):
        def where(i):
            return (0, which * per_part + jnp.clip(i - part * per_part, 0, per_part - 1), 0)

        return pl.BlockSpec((chunks, tile, LANES), where)

    my_targets = lax.dynamic_slice_in_dim(targets, place * rows, rows, 0)
    late_args = [x for x in (c_pair[0], d_pair[0], c_pair[1], d_pair[1]) for _ in range(3)]
    found, keep, send = pl.pallas_call(
        functools.partial(
            head_kernel, rows, tile, turn_cosine_coefficients(5), 1.0 / math.sqrt(total_rows), bits_a, bits_b
        ),
        grid=(CHUNK // tile,),
        in_specs=[scalars, scalars]
        + [pl.BlockSpec((y.shape[0], rows, tile, LANES), lambda i: (0, 0, i, 0)) for y in (y_low, y_high)]
        + [late_part(part, which) for part in range(4) for which in range(3)],
        out_specs=[
            pl.BlockSpec((8, LANES), lambda i: (0, 0)),
            pl.BlockSpec((chunks, LANES, LANES), lambda i: (0, 0, 0)),
            pl.BlockSpec((chunks, LANES, LANES), lambda i: (0, 0, 0)),
        ],
        out_shape=[
            jax.ShapeDtypeStruct((8, LANES), f32),
            jax.ShapeDtypeStruct((chunks, LANES, LANES), f32),
            jax.ShapeDtypeStruct((chunks, LANES, LANES), f32),
        ],
        scratch_shapes=[
            pltpu.VMEM((chunks, rows, CHUNK, LANES), f32),
            pltpu.VMEM((rows, 8, LANES), f32),
            pltpu.VMEM((3, chunks, tile, LANES), f32),
        ],
        compiler_params=pltpu.CompilerParams(vmem_limit_bytes=48 * MIB),
        name="head",
    )(about_me, my_targets, y_low, y_high, *late_args)

    if not direct:
        grads = jnp.stack([keep, send], 1).reshape(feat_size, rows_size, mine, LANES)
        grads = jnp.take(grads, jnp.arange(feat_size) ^ place, axis=0)
        keep = lax.dynamic_index_in_dim(grads, core, 1, False)
        send = lax.dynamic_index_in_dim(grads, core ^ 1, 1, False)
    feature_grad, found = scatter_sum(keep, send, found)
    return found[0], feature_grad.reshape(-1)


def solution(mesh):
    in_specs = (
        P("rows", None),
        P("feat"),
        P("feat"),
        P("feat"),
        P("feat"),
        P("feat"),
        P("feat", None, None),
        P("feat"),
        P("rows"),
    )
    out_specs = (P("rows"), P(("feat", "rows")))
    return jax.shard_map(local, mesh=mesh, in_specs=in_specs, out_specs=out_specs, check_vma=False)
```

```python
import functools
import math

import jax
import jax.numpy as jnp
import numpy as np
from jax import lax
from jax.experimental import pallas as pl
from jax.experimental.pallas import tpu as pltpu
from jax.sharding import PartitionSpec as P

LANES = 128
CHUNK = 256
BOTH = ("feat", "rows")
MIB = 1024 * 1024


def hadamard(length):
    matrix = np.ones((1, 1), np.float32)
    while matrix.shape[0] < length:
        matrix = np.block([[matrix, matrix], [matrix, -matrix]])
    return matrix


def halves(values):
    high = values.astype(jnp.bfloat16)
    low = (values - high.astype(jnp.float32)).astype(jnp.bfloat16)
    return high, low


def swap(values, axis_name, bit):
    size = lax.axis_size(axis_name)
    return lax.ppermute(values, axis_name, [(i, i ^ bit) for i in range(size)])


def bits_of(axis_name):
    return [1 << i for i in reversed(range(lax.axis_size(axis_name).bit_length() - 1))]


def gather_ordered(piece):
    shape = piece.shape
    held = piece[None]
    for axis_name in BOTH:
        index = lax.axis_index(axis_name)
        for bit in bits_of(axis_name):
            other = swap(held, axis_name, bit)
            upper = (index & bit) != 0
            held = jnp.where(
                upper, jnp.stack([other, held], 1), jnp.stack([held, other], 1)
            ).reshape((-1,) + shape)
    return held


def after(value, *others):
    return lax.optimization_barrier((value, *others))[0]


def doubled(held, bit):
    return jnp.concatenate([held, swap(held, "feat", bit)], axis=0)


def place_of(distance, bits):
    place = 0
    for i, bit in enumerate(bits):
        place = place + (((distance >> (bit.bit_length() - 1)) & 1) << i)
    return place


def scatter_sum(keep, send, extra):
    terms = keep + swap(send, "rows", 1)
    bits = bits_of("feat")
    count, lanes = terms.shape[1:]
    terms = terms.reshape((2,) * len(bits) + (count, lanes))
    cut = count // 2
    parts = [terms[..., :cut, :], terms[..., cut:, :]]
    names = [list(bits), list(bits)]

    def exchange(part, left, bit, extra):
        axis = left.index(bit)
        left.remove(bit)
        keep = lax.index_in_dim(part, 0, axis, False)
        send = lax.index_in_dim(part, 1, axis, False).reshape(-1, lanes)
        if extra is None:
            return keep + swap(send, "feat", bit).reshape(keep.shape), None
        got = swap(jnp.concatenate([send, extra], axis=0), "feat", bit)
        return keep + got[: send.shape[0]].reshape(keep.shape), extra + got[send.shape[0] :]

    for bit_a, bit_b in ((1, 2), (2, 1)):
        parts[0], extra = exchange(parts[0], names[0], bit_a, extra)
        parts[1], _ = exchange(parts[1], names[1], bit_b, None)
    rest = jnp.concatenate(parts, axis=-2)
    for bit in list(reversed(names[0])):
        rest, extra = exchange(rest, names[0], bit, extra)
    return rest, extra


def odd_bits(value):
    value = value ^ (value >> 4)
    value = value ^ (value >> 2)
    return (value ^ (value >> 1)) & 1


def mix_kernel(rows, begin, bits_a, bits_b, me_ref, a_own, a_other, b_own, b_other, emb_ref, lane_ref, block_ref, out_ref, sign_ref, wide_ref, spread_ref):
    f32 = jnp.float32
    bf16 = jnp.bfloat16
    chunks = a_own.shape[0]
    width = emb_ref.shape[0]
    quarters = width // LANES
    here = LANES // quarters
    chunk = pl.program_id(0) + begin

    def flip(bits):
        return (1 - 2 * (bits & 1)).astype(f32)

    @pl.when(chunk == begin)
    def _():
        for c, ref in enumerate((a_own, a_other)):
            for p in range(chunks):
                top = (c * chunks + p) * here
                for q in range(quarters):
                    sign_ref[top : top + here, q * LANES : (q + 1) * LANES] = ref[
                        p, q * here : (q + 1) * here, :
                    ].astype(bf16)
        sums = jnp.dot(jnp.ones((16, sign_ref.shape[0]), bf16), sign_ref[...], preferred_element_type=f32)
        odd = 0.5 * sums - 2.0 * jnp.floor(0.25 * sums)
        row = lax.broadcasted_iota(jnp.int32, odd.shape, 0)
        column = lax.broadcasted_iota(jnp.int32, odd.shape, 1)
        odd = jnp.where((row < 2 * quarters) & ((row & (quarters - 1)) == column // LANES), 0.5 * odd, 0.0)
        rest = jnp.dot(odd.astype(bf16), emb_ref[...], preferred_element_type=f32)
        high = rest.astype(bf16).astype(f32)
        row = lax.broadcasted_iota(jnp.int32, rest.shape, 0)
        wide_ref[0:width, :] = emb_ref[...]
        wide_ref[width:, :] = jnp.zeros((LANES, wide_ref.shape[1]), bf16)
        wide_ref[width : width + 16, :] = jnp.where(row < quarters, high, rest - high).astype(bf16)

    pa = place_of(chunk, bits_a)
    pb = place_of(chunk, bits_b)
    major_me = me_ref[0] * here
    columns = []
    for ref in (a_own, a_other):
        source = ref[pa, 3 * LANES // 2 : 3 * LANES // 2 + 1, :].astype(jnp.int32)
        major = source >> 2
        low = here.bit_length() - 1
        code = major & (here - 1)
        for i, bit in enumerate(bits_a):
            code = code | (((major >> (low + bit.bit_length())) & 1) << (low + i))
        code = code | (((major >> low) & 1) << (low + len(bits_a)))
        code = code | ((source & 3) << 10) | ((lax.population_count(major & major_me) & 1) << 12)
        columns.append(jnp.broadcast_to(code.astype(f32), (LANES, LANES)).T)
    code = jnp.concatenate(columns, axis=0).astype(jnp.int32)
    lane = lax.broadcasted_iota(jnp.int32, (CHUNK, LANES), 1)
    tiles = [flip(lax.population_count(code & lane))]
    for shift in range(7, 10):
        turn = flip(code >> shift)
        tiles = tiles + [tile * turn for tile in tiles]
    signs = jnp.concatenate([tile.astype(bf16) for tile in tiles], axis=1)
    sums = jnp.dot(signs, sign_ref[...], preferred_element_type=f32)
    flip_me, flip_1, flip_2 = flip(code >> 12), flip(code >> 10), flip(code >> 11)
    turns = [flip_me, flip_me * flip_1, flip_me * flip_2, flip_me * flip_1 * flip_2]
    left = [
        (jnp.floor(0.25 * sums[:, q * LANES : (q + 1) * LANES]) * turns[q]).astype(bf16) for q in range(4)
    ]
    tail = flip_me * jnp.where((lane & 1) != 0, flip_1, 1.0) * jnp.where((lane & 2) != 0, flip_2, 1.0)
    left.append(jnp.where(lane < 8, tail, 0.0).astype(bf16))
    first = jnp.dot(jnp.concatenate(left, axis=1), wide_ref[...], preferred_element_type=f32)

    half = LANES // 2
    order = jnp.concatenate(
        [
            ref[p, LANES : LANES + half, :]
            for ref, p in ((a_own, pa), (b_own, pb), (a_other, pa), (b_other, pb))
        ],
        axis=0,
    ).astype(jnp.int32)
    gain = jnp.concatenate(
        [
            ref[pb, 0:LANES, :] * (1 - 2 * odd_bits((2 * chunk + c) & me_ref[0])).astype(f32)
            for c, ref in enumerate((b_own, b_other))
        ],
        axis=0,
    )
    for r in range(rows):
        columns = slice(r * LANES, (r + 1) * LANES)
        mixed = jnp.take_along_axis(first[:, columns], order, axis=1) * gain
        across = jnp.dot(
            jnp.concatenate(halves(mixed), axis=1), lane_ref[...], preferred_element_type=f32
        )
        high, low = halves(across)
        spread_ref[0:CHUNK, columns] = high
        spread_ref[CHUNK:, columns] = low
    result = jnp.dot(block_ref[...], spread_ref[...], preferred_element_type=f32)
    for r in range(rows):
        out_ref[0, r] = result[:, r * LANES : (r + 1) * LANES]


def turn_cosine_coefficients(degree):
    points = np.cos(np.pi * (np.arange(400) + 0.5) / 400)
    u = 0.5 * points
    fit = np.polynomial.chebyshev.Chebyshev.fit(u * u, np.cos(2 * np.pi * u), degree, domain=[0, 0.25])
    return [float(c) for c in fit.convert(kind=np.polynomial.Polynomial).coef]


def head_kernel(
    rows, tile, coefs, grad_scale, bits_a, bits_b, parts, me_ref, target_ref, *refs
):
    y_refs, late_refs, refs = refs[:parts], refs[parts : parts + 12], refs[parts + 12 :]
    pred_ref, keep_ref, send_ref, feat_ref, acc_ref, stage_ref = refs
    f32 = jnp.float32
    step = pl.program_id(0)
    steps = pl.num_programs(0)
    chunks = feat_ref.shape[0]
    per_part = steps // 4

    @pl.when(step == 0)
    def _():
        acc_ref[...] = jnp.zeros_like(acc_ref)

    for part in range(4):
        core, bits = part // 2, (bits_a, bits_b)[part % 2]

        @pl.when(step // per_part == part)
        def _():
            scale_ref, phase_ref, weight_ref = late_refs[3 * part : 3 * part + 3]
            for k in range(chunks):
                place = place_of(k, bits)
                shared = odd_bits((2 * k + core) & me_ref[0]) ^ odd_bits(me_ref[0])
                stage_ref[0, k] = scale_ref[place] * (1 - 2 * shared).astype(f32)
                stage_ref[1, k] = phase_ref[place]
                stage_ref[2, k] = weight_ref[place]

    for part in range(tile // 8):
        here = slice(part * 8, part * 8 + 8)
        for r in range(rows):
            values = [y_ref[k, r, here, :] for y_ref in y_refs for k in range(y_ref.shape[0])]
            width = 1
            while width < chunks:
                for k in range(chunks):
                    if not k & width:
                        a, b = values[k], values[k | width]
                        values[k], values[k | width] = a + b, a - b
                width *= 2
            acc = acc_ref[r]
            for k in range(chunks):
                turns = values[k] * stage_ref[0, k, here, :] + stage_ref[1, k, here, :]
                u = turns - jnp.round(turns)
                square = u * u
                cosine = jnp.full_like(square, coefs[-1])
                for c in coefs[-2::-1]:
                    cosine = cosine * square + c
                feat_ref[k, r, pl.ds(pl.multiple_of(step * tile + part * 8, 8), 8), :] = cosine
                acc = acc + cosine * stage_ref[2, k, here, :]
            acc_ref[r] = acc

    @pl.when(step == steps - 1)
    def _():
        residuals = []
        lane = lax.broadcasted_iota(jnp.int32, (1, LANES), 1)
        found = jnp.zeros((1, LANES), f32)
        for r in range(rows):
            total = jnp.sum(jnp.sum(acc_ref[r], axis=0, keepdims=True), axis=1, keepdims=True)
            found = found + jnp.where(lane == me_ref[1] + r, total, 0.0)
            residuals.append(jnp.broadcast_to((total - target_ref[r]) * grad_scale, (8, LANES)))
        pred_ref[...] = jnp.broadcast_to(found, (8, LANES))

        for half, out_ref in enumerate((keep_ref, send_ref)):
            for k in range(chunks):

                @pl.loop(0, LANES // 32)
                def _(i):
                    for j in range(4):
                        row = pl.multiple_of(i * 32 + j * 8, 8)
                        rows_here = pl.ds(row + half * LANES, 8)
                        total = feat_ref[k, 0, rows_here, :] * residuals[0]
                        for r in range(1, rows):
                            total = total + feat_ref[k, r, rows_here, :] * residuals[r]
                        out_ref[k, pl.ds(row, 8), :] = total


def local(
    embeddings,
    sign_flips,
    gaussian,
    scales,
    phases,
    source_blocks,
    block_permutations,
    weights,
    targets,
):
    f32 = jnp.float32
    feat_size = lax.axis_size("feat")
    rows_size = lax.axis_size("rows")
    place = lax.axis_index("feat")
    core = lax.axis_index("rows")
    devices = feat_size * rows_size
    width = embeddings.shape[1]
    rows = embeddings.shape[0] // feat_size
    total_rows = embeddings.shape[0] * rows_size
    features = sign_flips.shape[0] * feat_size
    blocks = features // LANES
    mine = blocks // devices
    quarters = width // LANES
    chunks = blocks // CHUNK
    per_chunk = CHUNK // mine

    def half(values):
        parts = values.reshape((rows_size, values.shape[0] // rows_size) + values.shape[1:])
        return lax.dynamic_index_in_dim(parts, core, 0, False)

    def rows_of(*vectors):
        return jnp.concatenate([half(v) for v in vectors]).reshape(len(vectors), mine, LANES)

    positions = jnp.einsum(
        "bij,j->bi", half(block_permutations), jnp.arange(LANES).astype(jnp.bfloat16), preferred_element_type=f32
    )
    signs, gains = rows_of(sign_flips, gaussian)
    numbers = half(source_blocks).astype(f32)
    late = rows_of(
        scales * f32(4.0 / (2.0 * math.pi * features)),
        phases * f32(1.0 / (2.0 * math.pi)),
        weights * f32(1.0 / math.sqrt(features)),
    )
    bits = bits_of("feat")
    numbers = jnp.broadcast_to(jnp.pad(numbers, (0, LANES - mine))[None, :], (8, LANES))
    everything = [signs, positions, gains, *late, numbers]
    direct = mine == LANES and feat_size == chunks and rows_size == 2
    if direct:
        me = place * rows_size + core
        bits_a = bits[:-2] + [2, 1]
        bits_b = bits[:-2] + [1, 2]
    else:
        me = 0
        bits_a = bits_b = [1 << i for i in range(chunks.bit_length() - 1)]
        whole = gather_ordered(jnp.concatenate(everything))
        numbers = whole[:, 6 * mine, :mine].reshape(chunks, 2, 1, LANES)
        numbers = jnp.broadcast_to(numbers, (chunks, 2, 8, LANES))
        everything = [whole[:, i * mine : (i + 1) * mine].reshape(chunks, 2, LANES, LANES) for i in range(6)]
        everything.append(numbers)
    signs, positions, gains, *late, numbers = everything

    per_half = LANES // quarters
    shape = signs.shape
    signs = jnp.swapaxes(signs.reshape(shape[:-2] + (per_half, quarters, LANES)), -3, -2).reshape(shape)
    cut = LANES // 2
    pieces = [
        jnp.concatenate([signs, positions[..., :cut, :], numbers], axis=-2),
        jnp.concatenate([gains, positions[..., cut:, :]], axis=-2),
        jnp.concatenate([x[..., :cut, :] for x in late], axis=-2),
        jnp.concatenate([x[..., cut:, :] for x in late], axis=-2),
    ]
    if direct:
        early = [x[None] for x in pieces[:2]]
        late = [x[None] for x in pieces[2:]]
        for i in range(len(bits)):
            if i == len(bits) - 2:
                late = [after(x, *early) for x in late]
            if i >= len(bits) - 2:
                late = [doubled(x, bits[i + 2 - len(bits)]) for x in late]
            early = [doubled(x, b[i]) for x, b in zip(early, (bits_a, bits_b))]
            if i >= len(bits) - 2:
                early = [after(x, *late) for x in early]
        for i in range(2, len(bits) - 2):
            late = [doubled(x, bits[i]) for x in late]
        late = [after(x, *early) for x in late]
        late_got = [swap(x, "feat", b[-2]) for x, b in zip(late, (bits_a, bits_b))]
        a_pair, b_pair = ((x, swap(x, "rows", 1)) for x in early)
    else:
        a_pair, b_pair, c_pair, d_pair = ((x[:, 0], x[:, 1]) for x in pieces)

    emb = lax.dynamic_slice_in_dim(embeddings, place * rows, rows, 0)
    lane_signs = hadamard(LANES)
    emb = (emb.T.reshape(quarters, LANES, rows, 1) * jnp.asarray(lane_signs, jnp.bfloat16)[None, :, None, :]).reshape(
        width, rows * LANES
    )
    lane_matrix = jnp.asarray(np.concatenate([lane_signs] * 2, 0), jnp.bfloat16)
    block_matrix = jnp.asarray(np.concatenate([hadamard(CHUNK)] * 2, 1), jnp.bfloat16)
    about_me = jnp.stack([jnp.asarray(me, jnp.int32), (place * rows).astype(jnp.int32)])

    def resident(array):
        return pl.BlockSpec(array.shape, lambda k: (0,) * array.ndim)

    scalars = pl.BlockSpec(memory_space=pltpu.SMEM)
    resident_args = (*a_pair, *b_pair, emb, lane_matrix, block_matrix)

    def mix(begin, count):
        return pl.pallas_call(
            functools.partial(mix_kernel, rows, begin, bits_a, bits_b),
            grid=(count,),
            in_specs=[scalars] + [resident(x) for x in resident_args],
            out_specs=pl.BlockSpec((1, rows, CHUNK, LANES), lambda k: (k, 0, 0, 0)),
            out_shape=jax.ShapeDtypeStruct((count, rows, CHUNK, LANES), f32),
            scratch_shapes=[
                pltpu.VMEM((blocks // quarters, width), jnp.bfloat16),
                pltpu.VMEM((width + LANES, rows * LANES), jnp.bfloat16),
                pltpu.VMEM((2 * CHUNK, rows * LANES), jnp.bfloat16),
            ],
            compiler_params=pltpu.CompilerParams(vmem_limit_bytes=48 * MIB),
            cost_estimate=pl.CostEstimate(
                flops=count * 2 * 256 * 8192 * 256, bytes_accessed=count * rows * CHUNK * LANES * 4, transcendentals=0
            ),
            name="mix",
        )(about_me, *resident_args)

    cuts = (0, chunks // 4, chunks * 3 // 4, chunks)
    spread = [mix(cuts[0], cuts[1] - cuts[0])]
    if direct:
        late = [jnp.concatenate([x, after(y, spread[0])], axis=0) for x, y in zip(late, late_got)]
        late_got = [swap(x, "feat", b[-1]) for x, b in zip(late, (bits_a, bits_b))]
    spread.append(mix(cuts[1], cuts[2] - cuts[1]))
    if direct:
        late = [jnp.concatenate([x, after(y, spread[1])], axis=0) for x, y in zip(late, late_got)]
        c_pair, d_pair = ((x, swap(x, "rows", 1)) for x in late)
    spread.append(mix(cuts[2], cuts[3] - cuts[2]))

    tile = 32
    per_part = cut // tile

    def late_part(part, which):
        def where(i):
            return (0, which * per_part + jnp.clip(i - part * per_part, 0, per_part - 1), 0)

        return pl.BlockSpec((chunks, tile, LANES), where)

    my_targets = lax.dynamic_slice_in_dim(targets, place * rows, rows, 0)
    late_args = [x for x in (c_pair[0], d_pair[0], c_pair[1], d_pair[1]) for _ in range(3)]
    found, keep, send = pl.pallas_call(
        functools.partial(
            head_kernel, rows, tile, turn_cosine_coefficients(5), 1.0 / math.sqrt(total_rows), bits_a, bits_b, len(spread)
        ),
        grid=(CHUNK // tile,),
        in_specs=[scalars, scalars]
        + [pl.BlockSpec((y.shape[0], rows, tile, LANES), lambda i: (0, 0, i, 0)) for y in spread]
        + [late_part(part, which) for part in range(4) for which in range(3)],
        out_specs=[
            pl.BlockSpec((8, LANES), lambda i: (0, 0)),
            pl.BlockSpec((chunks, LANES, LANES), lambda i: (0, 0, 0)),
            pl.BlockSpec((chunks, LANES, LANES), lambda i: (0, 0, 0)),
        ],
        out_shape=[
            jax.ShapeDtypeStruct((8, LANES), f32),
            jax.ShapeDtypeStruct((chunks, LANES, LANES), f32),
            jax.ShapeDtypeStruct((chunks, LANES, LANES), f32),
        ],
        scratch_shapes=[
            pltpu.VMEM((chunks, rows, CHUNK, LANES), f32),
            pltpu.VMEM((rows, 8, LANES), f32),
            pltpu.VMEM((3, chunks, tile, LANES), f32),
        ],
        compiler_params=pltpu.CompilerParams(vmem_limit_bytes=48 * MIB),
        name="head",
    )(about_me, my_targets, *spread, *late_args)

    if not direct:
        grads = jnp.stack([keep, send], 1).reshape(feat_size, rows_size, mine, LANES)
        grads = jnp.take(grads, jnp.arange(feat_size) ^ place, axis=0)
        keep = lax.dynamic_index_in_dim(grads, core, 1, False)
        send = lax.dynamic_index_in_dim(grads, core ^ 1, 1, False)
    feature_grad, found = scatter_sum(keep, send, found)
    return found[0], feature_grad.reshape(-1)


def solution(mesh):
    in_specs = (
        P("rows", None),
        P("feat"),
        P("feat"),
        P("feat"),
        P("feat"),
        P("feat"),
        P("feat", None, None),
        P("feat"),
        P("rows"),
    )
    out_specs = (P("rows"), P(("feat", "rows")))
    return jax.shard_map(local, mesh=mesh, in_specs=in_specs, out_specs=out_specs, check_vma=False)
```

```python
import functools
import math

import jax
import jax.numpy as jnp
import numpy as np
from jax import lax
from jax.experimental import pallas as pl
from jax.experimental.pallas import tpu as pltpu
from jax.sharding import PartitionSpec as P

LANES = 128
CHUNK = 256
BOTH = ("feat", "rows")
MIB = 1024 * 1024
VMEM_MIX = 16 * MIB
VMEM_HEAD = 20 * MIB


def hadamard(length):
    matrix = np.ones((1, 1), np.float32)
    while matrix.shape[0] < length:
        matrix = np.block([[matrix, matrix], [matrix, -matrix]])
    return matrix


def halves(values):
    high = values.astype(jnp.bfloat16)
    low = (values - high.astype(jnp.float32)).astype(jnp.bfloat16)
    return high, low


def swap(values, axis_name, bit):
    size = lax.axis_size(axis_name)
    return lax.ppermute(values, axis_name, [(i, i ^ bit) for i in range(size)])


def bits_of(axis_name):
    return [1 << i for i in reversed(range(lax.axis_size(axis_name).bit_length() - 1))]


def gather_ordered(piece):
    shape = piece.shape
    held = piece[None]
    for axis_name in BOTH:
        index = lax.axis_index(axis_name)
        for bit in bits_of(axis_name):
            other = swap(held, axis_name, bit)
            upper = (index & bit) != 0
            held = jnp.where(
                upper, jnp.stack([other, held], 1), jnp.stack([held, other], 1)
            ).reshape((-1,) + shape)
    return held


def after(value, *others):
    return lax.optimization_barrier((value, *others))[0]


def doubled(held, bit):
    return jnp.concatenate([held, swap(held, "feat", bit)], axis=0)


def place_of(distance, bits):
    place = 0
    for i, bit in enumerate(bits):
        place = place + (((distance >> (bit.bit_length() - 1)) & 1) << i)
    return place


def scatter_sum(keep, send, extra):
    terms = keep + swap(send, "rows", 1)
    bits = bits_of("feat")
    count, lanes = terms.shape[1:]
    terms = terms.reshape((2,) * len(bits) + (count, lanes))
    cut = count // 2
    parts = [terms[..., :cut, :], terms[..., cut:, :]]
    names = [list(bits), list(bits)]

    def exchange(part, left, bit, extra):
        axis = left.index(bit)
        left.remove(bit)
        keep = lax.index_in_dim(part, 0, axis, False)
        send = lax.index_in_dim(part, 1, axis, False).reshape(-1, lanes)
        if extra is None:
            return keep + swap(send, "feat", bit).reshape(keep.shape), None
        got = swap(jnp.concatenate([send, extra], axis=0), "feat", bit)
        return keep + got[: send.shape[0]].reshape(keep.shape), extra + got[send.shape[0] :]

    for bit_a, bit_b in ((1, 2), (2, 1)):
        parts[0], extra = exchange(parts[0], names[0], bit_a, extra)
        parts[1], _ = exchange(parts[1], names[1], bit_b, None)
    rest = jnp.concatenate(parts, axis=-2)
    for bit in list(reversed(names[0])):
        rest, extra = exchange(rest, names[0], bit, extra)
    return rest, extra


def odd_bits(value):
    value = value ^ (value >> 4)
    value = value ^ (value >> 2)
    return (value ^ (value >> 1)) & 1


def mix_kernel(rows, begin, group, bits_a, bits_b, me_ref, a_own, a_other, b_own, b_other, emb_ref, lane_ref, block_ref, out_ref, sign_ref, wide_ref, spread_ref):
    f32 = jnp.float32
    bf16 = jnp.bfloat16
    chunks = a_own.shape[0]
    width = emb_ref.shape[0]
    quarters = width // LANES
    here = LANES // quarters
    def flip(bits):
        return (1 - 2 * (bits & 1)).astype(f32)

    for c, ref in enumerate((a_own, a_other)):
        for p in range(chunks):
            top = (c * chunks + p) * here
            for q in range(quarters):
                sign_ref[top : top + here, q * LANES : (q + 1) * LANES] = ref[
                    p, q * here : (q + 1) * here, :
                ].astype(bf16)
    sums = jnp.dot(jnp.ones((16, sign_ref.shape[0]), bf16), sign_ref[...], preferred_element_type=f32)
    odd = 0.5 * sums - 2.0 * jnp.floor(0.25 * sums)
    row = lax.broadcasted_iota(jnp.int32, odd.shape, 0)
    column = lax.broadcasted_iota(jnp.int32, odd.shape, 1)
    odd = jnp.where((row < 2 * quarters) & ((row & (quarters - 1)) == column // LANES), 0.5 * odd, 0.0)
    rest = jnp.dot(odd.astype(bf16), emb_ref[...], preferred_element_type=f32)
    high = rest.astype(bf16).astype(f32)
    row = lax.broadcasted_iota(jnp.int32, rest.shape, 0)
    wide_ref[0:width, :] = emb_ref[...]
    wide_ref[width:, :] = jnp.zeros((LANES, wide_ref.shape[1]), bf16)
    wide_ref[width : width + 16, :] = jnp.where(row < quarters, high, rest - high).astype(bf16)

    major_me = me_ref[0] * here
    low = here.bit_length() - 1
    half = LANES // 2
    lane = lax.broadcasted_iota(jnp.int32, (CHUNK, LANES), 1)
    @pl.loop(0, out_ref.shape[0] // group)
    def _(step):
        left = []
        orders = []
        gains = []
        for g in range(group):
            chunk = begin + step * group + g
            pa = place_of(chunk, bits_a)
            pb = place_of(chunk, bits_b)
            columns = []
            for ref in (a_own, a_other):
                source = ref[pa, 3 * half : 3 * half + 1, :].astype(jnp.int32)
                major = source >> 2
                code = major & (here - 1)
                for i, bit in enumerate(bits_a):
                    code = code | (((major >> (low + bit.bit_length())) & 1) << (low + i))
                code = code | (((major >> low) & 1) << (low + len(bits_a)))
                code = code | ((source & 3) << 10) | ((lax.population_count(major & major_me) & 1) << 12)
                columns.append(jnp.broadcast_to(code.astype(f32), (LANES, LANES)).T)
            code = jnp.concatenate(columns, axis=0).astype(jnp.int32)
            tiles = [flip(lax.population_count(code & lane))]
            for shift in range(7, 10):
                turn = flip(code >> shift)
                tiles = tiles + [tile * turn for tile in tiles]
            signs = jnp.concatenate([tile.astype(bf16) for tile in tiles], axis=1)
            sums = jnp.dot(signs, sign_ref[...], preferred_element_type=f32)
            flip_me, flip_1, flip_2 = flip(code >> 12), flip(code >> 10), flip(code >> 11)
            turns = [flip_me, flip_me * flip_1, flip_me * flip_2, flip_me * flip_1 * flip_2]
            parts = [
                (jnp.floor(0.25 * sums[:, q * LANES : (q + 1) * LANES]) * turns[q]).astype(bf16) for q in range(4)
            ]
            tail = flip_me * jnp.where((lane & 1) != 0, flip_1, 1.0) * jnp.where((lane & 2) != 0, flip_2, 1.0)
            parts.append(jnp.where(lane < 8, tail, 0.0).astype(bf16))
            left.append(jnp.concatenate(parts, axis=1))
            orders.append(
                jnp.concatenate(
                    [
                        ref[p, LANES : LANES + half, :]
                        for ref, p in ((a_own, pa), (b_own, pb), (a_other, pa), (b_other, pb))
                    ],
                    axis=0,
                ).astype(jnp.int32)
            )
            gains.append(
                jnp.concatenate(
                    [
                        ref[pb, 0:LANES, :] * (1 - 2 * odd_bits((2 * chunk + c) & me_ref[0])).astype(f32)
                        for c, ref in enumerate((b_own, b_other))
                    ],
                    axis=0,
                )
            )
        order = jnp.concatenate(orders, axis=0)
        gain = jnp.concatenate(gains, axis=0)
        first = jnp.dot(jnp.concatenate(left, axis=0), wide_ref[...], preferred_element_type=f32)
        for r in range(rows):
            columns = slice(r * LANES, (r + 1) * LANES)
            mixed = jnp.take_along_axis(first[:, columns], order, axis=1) * gain
            across = jnp.dot(
                jnp.concatenate(halves(mixed), axis=1), lane_ref[...], preferred_element_type=f32
            )
            high, low_part = halves(across)
            for g in range(group):
                here_rows = slice(g * CHUNK, (g + 1) * CHUNK)
                spread_ref[g, 0:CHUNK, columns] = high[here_rows]
                spread_ref[g, CHUNK:, columns] = low_part[here_rows]
        for g in range(group):
            result = jnp.dot(block_ref[...], spread_ref[g], preferred_element_type=f32)
            for r in range(rows):
                out_ref[step * group + g, r] = result[:, r * LANES : (r + 1) * LANES]


def turn_cosine_coefficients(degree):
    points = np.cos(np.pi * (np.arange(400) + 0.5) / 400)
    u = 0.5 * points
    fit = np.polynomial.chebyshev.Chebyshev.fit(u * u, np.cos(2 * np.pi * u), degree, domain=[0, 0.25])
    return [float(c) for c in fit.convert(kind=np.polynomial.Polynomial).coef]


def head_kernel(rows, coefs, grad_scale, bits_a, bits_b, parts, me_ref, target_ref, *refs):
    y_refs, late_refs, refs = refs[:parts], refs[parts : parts + 4], refs[parts + 4 :]
    pred_ref, keep_ref, send_ref, feat_ref, acc_ref, scale_ref = refs
    f32 = jnp.float32
    chunks = feat_ref.shape[0]
    cut = LANES // 2
    acc_ref[...] = jnp.zeros_like(acc_ref)

    for part, late_ref in enumerate(late_refs):
        core, bits = part // 2, (bits_a, bits_b)[part % 2]
        turns_me = [
            (1 - 2 * (odd_bits((2 * k + core) & me_ref[0]) ^ odd_bits(me_ref[0]))).astype(f32)
            for k in range(chunks)
        ]

        @pl.loop(0, cut // 8)
        def _(i):
            row = pl.multiple_of(i * 8, 8)
            here = pl.ds(row + part * cut, 8)
            for k in range(chunks):
                scale_ref[k] = late_ref[place_of(k, bits), pl.ds(row, 8), :] * turns_me[k]
            for r in range(rows):
                values = [y_ref[k, r, here, :] for y_ref in y_refs for k in range(y_ref.shape[0])]
                width = 1
                while width < chunks:
                    for k in range(chunks):
                        if not k & width:
                            a, b = values[k], values[k | width]
                            values[k], values[k | width] = a + b, a - b
                    width *= 2
                acc = acc_ref[r]
                for k in range(chunks):
                    place = place_of(k, bits)
                    turns = values[k] * scale_ref[k] + late_ref[place, pl.ds(row + cut, 8), :]
                    u = turns - jnp.round(turns)
                    square = u * u
                    cosine = jnp.full_like(square, coefs[-1])
                    for c in coefs[-2::-1]:
                        cosine = cosine * square + c
                    feat_ref[k, r, here, :] = cosine
                    acc = acc + cosine * late_ref[place, pl.ds(row + 2 * cut, 8), :]
                acc_ref[r] = acc

    residuals = []
    lane = lax.broadcasted_iota(jnp.int32, (1, LANES), 1)
    found = jnp.zeros((1, LANES), f32)
    for r in range(rows):
        total = jnp.sum(jnp.sum(acc_ref[r], axis=0, keepdims=True), axis=1, keepdims=True)
        found = found + jnp.where(lane == me_ref[1] + r, total, 0.0)
        residuals.append(jnp.broadcast_to((total - target_ref[r]) * grad_scale, (8, LANES)))
    pred_ref[...] = jnp.broadcast_to(found, (8, LANES))

    for half, out_ref in enumerate((keep_ref, send_ref)):

        @pl.loop(0, LANES // 8)
        def _(i):
            row = pl.multiple_of(i * 8, 8)
            rows_here = pl.ds(row + half * LANES, 8)
            for k in range(chunks):
                total = feat_ref[k, 0, rows_here, :] * residuals[0]
                for r in range(1, rows):
                    total = total + feat_ref[k, r, rows_here, :] * residuals[r]
                out_ref[k, pl.ds(row, 8), :] = total


def local(
    embeddings,
    sign_flips,
    gaussian,
    scales,
    phases,
    source_blocks,
    block_permutations,
    weights,
    targets,
):
    f32 = jnp.float32
    feat_size = lax.axis_size("feat")
    rows_size = lax.axis_size("rows")
    place = lax.axis_index("feat")
    core = lax.axis_index("rows")
    devices = feat_size * rows_size
    width = embeddings.shape[1]
    rows = embeddings.shape[0] // feat_size
    total_rows = embeddings.shape[0] * rows_size
    features = sign_flips.shape[0] * feat_size
    blocks = features // LANES
    mine = blocks // devices
    quarters = width // LANES
    chunks = blocks // CHUNK
    per_chunk = CHUNK // mine

    def half(values):
        parts = values.reshape((rows_size, values.shape[0] // rows_size) + values.shape[1:])
        return lax.dynamic_index_in_dim(parts, core, 0, False)

    def rows_of(*vectors):
        return jnp.concatenate([half(v) for v in vectors]).reshape(len(vectors), mine, LANES)

    positions = jnp.einsum(
        "bij,j->bi", half(block_permutations), jnp.arange(LANES).astype(jnp.bfloat16), preferred_element_type=f32
    )
    signs, gains = rows_of(sign_flips, gaussian)
    numbers = half(source_blocks).astype(f32)
    late = rows_of(
        scales * f32(4.0 / (2.0 * math.pi * features)),
        phases * f32(1.0 / (2.0 * math.pi)),
        weights * f32(1.0 / math.sqrt(features)),
    )
    bits = bits_of("feat")
    numbers = jnp.broadcast_to(jnp.pad(numbers, (0, LANES - mine))[None, :], (8, LANES))
    everything = [signs, positions, gains, *late, numbers]
    direct = mine == LANES and feat_size == chunks and rows_size == 2
    if direct:
        me = place * rows_size + core
        bits_a = bits[:-2] + [2, 1]
        bits_b = bits[:-2] + [1, 2]
    else:
        me = 0
        bits_a = bits_b = [1 << i for i in range(chunks.bit_length() - 1)]
        whole = gather_ordered(jnp.concatenate(everything))
        numbers = whole[:, 6 * mine, :mine].reshape(chunks, 2, 1, LANES)
        numbers = jnp.broadcast_to(numbers, (chunks, 2, 8, LANES))
        everything = [whole[:, i * mine : (i + 1) * mine].reshape(chunks, 2, LANES, LANES) for i in range(6)]
        everything.append(numbers)
    signs, positions, gains, *late, numbers = everything

    per_half = LANES // quarters
    shape = signs.shape
    signs = jnp.swapaxes(signs.reshape(shape[:-2] + (per_half, quarters, LANES)), -3, -2).reshape(shape)
    cut = LANES // 2
    pieces = [
        jnp.concatenate([signs, positions[..., :cut, :], numbers], axis=-2),
        jnp.concatenate([gains, positions[..., cut:, :]], axis=-2),
        jnp.concatenate([x[..., :cut, :] for x in late], axis=-2),
        jnp.concatenate([x[..., cut:, :] for x in late], axis=-2),
    ]
    if direct:
        early = [x[None] for x in pieces[:2]]
        late = [x[None] for x in pieces[2:]]
        for i in range(len(bits)):
            if i == len(bits) - 2:
                late = [after(x, *early) for x in late]
            if i >= len(bits) - 2:
                late = [doubled(x, bits[i + 2 - len(bits)]) for x in late]
            early = [doubled(x, b[i]) for x, b in zip(early, (bits_a, bits_b))]
            if i >= len(bits) - 2:
                early = [after(x, *late) for x in early]
        for i in range(2, len(bits) - 2):
            late = [doubled(x, bits[i]) for x in late]
        late = [after(x, *early) for x in late]
        late_got = [swap(x, "feat", b[-2]) for x, b in zip(late, (bits_a, bits_b))]
        a_pair, b_pair = ((x, swap(x, "rows", 1)) for x in early)
    else:
        a_pair, b_pair, c_pair, d_pair = ((x[:, 0], x[:, 1]) for x in pieces)

    emb = lax.dynamic_slice_in_dim(embeddings, place * rows, rows, 0)
    lane_signs = hadamard(LANES)
    emb = (emb.T.reshape(quarters, LANES, rows, 1) * jnp.asarray(lane_signs, jnp.bfloat16)[None, :, None, :]).reshape(
        width, rows * LANES
    )
    lane_matrix = jnp.asarray(np.concatenate([lane_signs] * 2, 0), jnp.bfloat16)
    block_matrix = jnp.asarray(np.concatenate([hadamard(CHUNK)] * 2, 1), jnp.bfloat16)
    about_me = jnp.stack([jnp.asarray(me, jnp.int32), (place * rows).astype(jnp.int32)])

    scalars = pl.BlockSpec(memory_space=pltpu.SMEM)
    vmem = pl.BlockSpec(memory_space=pltpu.VMEM)
    resident_args = (*a_pair, *b_pair, emb, lane_matrix, block_matrix)

    def mix(begin, count, group=2):
        return pl.pallas_call(
            functools.partial(mix_kernel, rows, begin, group, bits_a, bits_b),
            in_specs=[scalars] + [vmem] * len(resident_args),
            out_specs=vmem,
            out_shape=jax.ShapeDtypeStruct((count, rows, CHUNK, LANES), f32),
            scratch_shapes=[
                pltpu.VMEM((blocks // quarters, width), jnp.bfloat16),
                pltpu.VMEM((width + LANES, rows * LANES), jnp.bfloat16),
                pltpu.VMEM((group, 2 * CHUNK, rows * LANES), jnp.bfloat16),
            ],
            compiler_params=pltpu.CompilerParams(vmem_limit_bytes=VMEM_MIX),
            cost_estimate=pl.CostEstimate(
                flops=count * 2 * 256 * 8192 * 256, bytes_accessed=count * rows * CHUNK * LANES * 4, transcendentals=0
            ),
            name="mix",
        )(about_me, *resident_args)

    cuts = (0, chunks // 4, chunks * 3 // 4, chunks)
    spread = [mix(cuts[0], cuts[1] - cuts[0])]
    if direct:
        late = [jnp.concatenate([x, after(y, spread[0])], axis=0) for x, y in zip(late, late_got)]
        late_got = [swap(x, "feat", b[-1]) for x, b in zip(late, (bits_a, bits_b))]
    spread.append(mix(cuts[1], cuts[2] - cuts[1]))
    if direct:
        late = [jnp.concatenate([x, after(y, spread[1])], axis=0) for x, y in zip(late, late_got)]
        c_pair, d_pair = ((x, swap(x, "rows", 1)) for x in late)
    spread.append(mix(cuts[2], cuts[3] - cuts[2]))

    my_targets = lax.dynamic_slice_in_dim(targets, place * rows, rows, 0)
    found, keep, send = pl.pallas_call(
        functools.partial(
            head_kernel, rows, turn_cosine_coefficients(5), 1.0 / math.sqrt(total_rows), bits_a, bits_b, len(spread)
        ),
        in_specs=[scalars, scalars] + [vmem] * (len(spread) + 4),
        out_specs=[vmem] * 3,
        out_shape=[
            jax.ShapeDtypeStruct((8, LANES), f32),
            jax.ShapeDtypeStruct((chunks, LANES, LANES), f32),
            jax.ShapeDtypeStruct((chunks, LANES, LANES), f32),
        ],
        scratch_shapes=[
            pltpu.VMEM((chunks, rows, CHUNK, LANES), f32),
            pltpu.VMEM((rows, 8, LANES), f32),
            pltpu.VMEM((chunks, 8, LANES), f32),
        ],
        compiler_params=pltpu.CompilerParams(vmem_limit_bytes=VMEM_HEAD),
        name="head",
    )(about_me, my_targets, *spread, c_pair[0], d_pair[0], c_pair[1], d_pair[1])

    if not direct:
        grads = jnp.stack([keep, send], 1).reshape(feat_size, rows_size, mine, LANES)
        grads = jnp.take(grads, jnp.arange(feat_size) ^ place, axis=0)
        keep = lax.dynamic_index_in_dim(grads, core, 1, False)
        send = lax.dynamic_index_in_dim(grads, core ^ 1, 1, False)
    feature_grad, found = scatter_sum(keep, send, found)
    return found[0], feature_grad.reshape(-1)


def solution(mesh):
    in_specs = (
        P("rows", None),
        P("feat"),
        P("feat"),
        P("feat"),
        P("feat"),
        P("feat"),
        P("feat", None, None),
        P("feat"),
        P("rows"),
    )
    out_specs = (P("rows"), P(("feat", "rows")))
    return jax.shard_map(local, mesh=mesh, in_specs=in_specs, out_specs=out_specs, check_vma=False)
```

```python
import functools
import math

import jax
import jax.numpy as jnp
import numpy as np
from jax import lax
from jax.experimental import pallas as pl
from jax.experimental.pallas import tpu as pltpu
from jax.sharding import PartitionSpec as P

LANES = 128
CHUNK = 256
BOTH = ("feat", "rows")
MIB = 1024 * 1024
VMEM_MIX = 16 * MIB
VMEM_HEAD = 20 * MIB
LITTLE = pl.CostEstimate(flops=1, bytes_accessed=1, transcendentals=0)


def hadamard(length):
    matrix = np.ones((1, 1), np.float32)
    while matrix.shape[0] < length:
        matrix = np.block([[matrix, matrix], [matrix, -matrix]])
    return matrix


def halves(values):
    high = values.astype(jnp.bfloat16)
    low = (values - high.astype(jnp.float32)).astype(jnp.bfloat16)
    return high, low


def swap(values, axis_name, bit):
    size = lax.axis_size(axis_name)
    return lax.ppermute(values, axis_name, [(i, i ^ bit) for i in range(size)])


def bits_of(axis_name):
    return [1 << i for i in reversed(range(lax.axis_size(axis_name).bit_length() - 1))]


def gather_ordered(piece):
    shape = piece.shape
    held = piece[None]
    for axis_name in BOTH:
        index = lax.axis_index(axis_name)
        for bit in bits_of(axis_name):
            other = swap(held, axis_name, bit)
            upper = (index & bit) != 0
            held = jnp.where(
                upper, jnp.stack([other, held], 1), jnp.stack([held, other], 1)
            ).reshape((-1,) + shape)
    return held


def after(value, *others):
    return lax.optimization_barrier((value, *others))[0]


def doubled(held, bit):
    return jnp.concatenate([held, swap(held, "feat", bit)], axis=0)


def place_of(distance, bits):
    place = 0
    for i, bit in enumerate(bits):
        place = place + (((distance >> (bit.bit_length() - 1)) & 1) << i)
    return place


def scatter_sum(keep, send, extra):
    terms = keep + swap(send, "rows", 1)
    bits = bits_of("feat")
    count, lanes = terms.shape[1:]
    terms = terms.reshape((2,) * len(bits) + (count, lanes))
    cut = count // 2
    parts = [terms[..., :cut, :], terms[..., cut:, :]]
    names = [list(bits), list(bits)]

    def exchange(part, left, bit, extra):
        axis = left.index(bit)
        left.remove(bit)
        keep = lax.index_in_dim(part, 0, axis, False)
        send = lax.index_in_dim(part, 1, axis, False).reshape(-1, lanes)
        if extra is None:
            return keep + swap(send, "feat", bit).reshape(keep.shape), None
        got = swap(jnp.concatenate([send, extra], axis=0), "feat", bit)
        return keep + got[: send.shape[0]].reshape(keep.shape), extra + got[send.shape[0] :]

    for bit_a, bit_b in ((1, 2), (2, 1)):
        parts[0], extra = exchange(parts[0], names[0], bit_a, extra)
        parts[1], _ = exchange(parts[1], names[1], bit_b, None)
    rest = jnp.concatenate(parts, axis=-2)
    for bit in list(reversed(names[0])):
        rest, extra = exchange(rest, names[0], bit, extra)
    return rest, extra


def odd_bits(value):
    value = value ^ (value >> 4)
    value = value ^ (value >> 2)
    return (value ^ (value >> 1)) & 1


def flip(bits):
    return (1 - 2 * (bits & 1)).astype(jnp.float32)


def prepare(bits_a, bits_b, a_own, a_other, b_own, b_other, emb_ref, sign_ref, wide_ref):
    f32 = jnp.float32
    bf16 = jnp.bfloat16
    chunks = a_own.shape[0]
    width = emb_ref.shape[0]
    quarters = width // LANES
    here = LANES // quarters
    few = here // 2
    order = [place_of(distance, bits_a) for distance in range(chunks)]

    for c, pair in enumerate(((a_own, b_own), (a_other, b_other))):
        for part, (ref, bits) in enumerate(zip(pair, (bits_a, bits_b))):
            for distance in range(chunks):
                top = (c * chunks + order[distance]) * here + part * few
                for q in range(quarters):
                    sign_ref[top : top + few, q * LANES : (q + 1) * LANES] = ref[
                        place_of(distance, bits), q * few : (q + 1) * few, :
                    ].astype(bf16)
    sums = jnp.dot(jnp.ones((16, sign_ref.shape[0]), bf16), sign_ref[...], preferred_element_type=f32)
    odd = 0.5 * sums - 2.0 * jnp.floor(0.25 * sums)
    row = lax.broadcasted_iota(jnp.int32, odd.shape, 0)
    column = lax.broadcasted_iota(jnp.int32, odd.shape, 1)
    odd = jnp.where((row < 2 * quarters) & ((row & (quarters - 1)) == column // LANES), 0.5 * odd, 0.0)
    rest = jnp.dot(odd.astype(bf16), emb_ref[...], preferred_element_type=f32)
    high = rest.astype(bf16).astype(f32)
    row = lax.broadcasted_iota(jnp.int32, rest.shape, 0)
    wide_ref[0:width, :] = emb_ref[...]
    wide_ref[width:, :] = jnp.zeros((LANES, wide_ref.shape[1]), bf16)
    wide_ref[width : width + 16, :] = jnp.where(row < quarters, high, rest - high).astype(bf16)


def first_kernel(rows, begin, group, bits_a, bits_b, me_ref, a_own, a_other, b_own, b_other, *refs):
    f32 = jnp.float32
    bf16 = jnp.bfloat16
    if begin == 0:
        emb_ref, out_ref, sign_ref, wide_ref = refs
        prepare(bits_a, bits_b, a_own, a_other, b_own, b_other, emb_ref, sign_ref, wide_ref)
    else:
        sign_ref, wide_ref, out_ref = refs
    here = sign_ref.shape[0] // (2 * a_own.shape[0])
    major_me = me_ref[0] * here
    low = here.bit_length() - 1
    lane = lax.broadcasted_iota(jnp.int32, (CHUNK, LANES), 1)

    @pl.loop(0, out_ref.shape[0] // group)
    def _(step):
        left = []
        for g in range(group):
            pa = place_of(begin + step * group + g, bits_a)
            columns = []
            for ref in (a_own, a_other):
                source = ref[pa, LANES // 2 : LANES // 2 + 1, :].astype(jnp.int32)
                major = source >> 2
                code = major & (here - 1)
                for i, bit in enumerate(bits_a):
                    code = code | (((major >> (low + bit.bit_length())) & 1) << (low + i))
                code = code | (((major >> low) & 1) << (low + len(bits_a)))
                code = code | ((source & 3) << 10) | ((lax.population_count(major & major_me) & 1) << 12)
                columns.append(jnp.broadcast_to(code.astype(f32), (LANES, LANES)).T)
            code = jnp.concatenate(columns, axis=0).astype(jnp.int32)
            tiles = [flip(lax.population_count(code & lane))]
            for shift in range(7, 10):
                turn = flip(code >> shift)
                tiles = tiles + [tile * turn for tile in tiles]
            signs = jnp.concatenate([tile.astype(bf16) for tile in tiles], axis=1)
            sums = jnp.dot(signs, sign_ref[...], preferred_element_type=f32)
            flip_me, flip_1, flip_2 = flip(code >> 12), flip(code >> 10), flip(code >> 11)
            turns = [flip_me, flip_me * flip_1, flip_me * flip_2, flip_me * flip_1 * flip_2]
            parts = [
                (jnp.floor(0.25 * sums[:, q * LANES : (q + 1) * LANES]) * turns[q]).astype(bf16)
                for q in range(4)
            ]
            tail = flip_me * jnp.where((lane & 1) != 0, flip_1, 1.0) * jnp.where((lane & 2) != 0, flip_2, 1.0)
            parts.append(jnp.where(lane < 8, tail, 0.0).astype(bf16))
            left.append(jnp.concatenate(parts, axis=1))
        first = jnp.dot(jnp.concatenate(left, axis=0), wide_ref[...], preferred_element_type=f32)
        for g in range(group):
            for r in range(rows):
                out_ref[step * group + g, r] = first[g * CHUNK : (g + 1) * CHUNK, r * LANES : (r + 1) * LANES]


def mix_kernel(rows, begin, group, bits_a, bits_b, me_ref, first_ref, *refs):
    a_refs, b_refs, (lane_ref, block_ref, out_ref, spread_ref) = refs[:4], refs[4:8], refs[8:]
    f32 = jnp.float32
    top = max(bits_a[-1], bits_b[-1])

    def piece(refs, core, chunk, within, bits):
        far = 1 if within & bits[-1] else 0
        return refs[2 * core + far][place_of(chunk, bits[:-1])]

    @pl.loop(0, out_ref.shape[0] // (2 * top))
    def _(step):
        for within in range(0, 2 * top, group):
            at = step * 2 * top + within
            orders = []
            gains = []
            for g in range(group):
                chunk = begin + at + g
                orders += [piece(a_refs, c, chunk, within + g, bits_a) for c in range(2)]
                gains += [
                    piece(b_refs, c, chunk, within + g, bits_b)
                    * (1 - 2 * odd_bits((2 * chunk + c) & me_ref[0])).astype(f32)
                    for c in range(2)
                ]
            order = jnp.concatenate(orders, axis=0).astype(jnp.int32)
            gain = jnp.concatenate(gains, axis=0)
            for r in range(rows):
                columns = slice(r * LANES, (r + 1) * LANES)
                first = jnp.concatenate([first_ref[at + g, r] for g in range(group)], axis=0)
                mixed = jnp.take_along_axis(first, order, axis=1) * gain
                across = jnp.dot(
                    jnp.concatenate(halves(mixed), axis=1), lane_ref[...], preferred_element_type=f32
                )
                high, low = halves(across)
                for g in range(group):
                    here = slice(g * CHUNK, (g + 1) * CHUNK)
                    spread_ref[g, 0:CHUNK, columns] = high[here]
                    spread_ref[g, CHUNK:, columns] = low[here]
            for g in range(group):
                result = jnp.dot(block_ref[...], spread_ref[g], preferred_element_type=f32)
                for r in range(rows):
                    out_ref[at + g, r] = result[:, r * LANES : (r + 1) * LANES]


def turn_sine_coefficients(degree):
    points = np.cos(np.pi * (np.arange(400) + 0.5) / 400)
    v = 0.125 + 0.125 * points
    fit = np.polynomial.chebyshev.Chebyshev.fit(
        v * v, np.sin(2 * np.pi * v) / v, degree, domain=[0, 0.0625], w=v
    )
    return [float(c) for c in fit.convert(kind=np.polynomial.Polynomial).coef]


def head_kernel(rows, coefs, grad_scale, bits_a, bits_b, parts, me_ref, target_ref, *refs):
    y_refs, late_refs, refs = refs[:parts], refs[parts : parts + 8], refs[parts + 8 :]
    pred_ref, keep_ref, send_ref, feat_ref, acc_ref, scale_ref = refs
    f32 = jnp.float32
    chunks = feat_ref.shape[0]
    cut = LANES // 2
    acc_ref[...] = jnp.zeros_like(acc_ref)

    for part in range(4):
        core, bits = part // 2, (bits_a, bits_b)[part % 2]
        near = late_refs[2 * part].shape[0]
        late = [late_refs[2 * part + place // near].at[place % near] for place in range(chunks)]
        turns_me = [
            (1 - 2 * (odd_bits((2 * k + core) & me_ref[0]) ^ odd_bits(me_ref[0]))).astype(f32)
            for k in range(chunks)
        ]

        @pl.loop(0, cut // 8)
        def _(i):
            row = pl.multiple_of(i * 8, 8)
            here = pl.ds(row + part * cut, 8)
            for k in range(chunks):
                scale_ref[k] = late[place_of(k, bits)][pl.ds(row, 8), :] * turns_me[k]
            for r in range(rows):
                values = [y_ref[k, r, here, :] for y_ref in y_refs for k in range(y_ref.shape[0])]
                width = 1
                while width < chunks:
                    for k in range(chunks):
                        if not k & width:
                            a, b = values[k], values[k | width]
                            values[k], values[k | width] = a + b, a - b
                    width *= 2
                acc = acc_ref[r]
                for k in range(chunks):
                    place = place_of(k, bits)
                    turns = values[k] * scale_ref[k] + late[place][pl.ds(row + cut, 8), :]
                    quarter = 0.25 - jnp.abs(turns - jnp.round(turns))
                    square = quarter * quarter
                    cosine = square * coefs[-1] + coefs[-2]
                    for c in coefs[-3::-1]:
                        cosine = cosine * square + c
                    cosine = cosine * quarter
                    feat_ref[k, r, here, :] = cosine
                    acc = acc + cosine * late[place][pl.ds(row + 2 * cut, 8), :]
                acc_ref[r] = acc

    residuals = []
    lane = lax.broadcasted_iota(jnp.int32, (1, LANES), 1)
    found = jnp.zeros((1, LANES), f32)
    for r in range(rows):
        total = jnp.sum(jnp.sum(acc_ref[r], axis=0, keepdims=True), axis=1, keepdims=True)
        found = found + jnp.where(lane == me_ref[1] + r, total, 0.0)
        residuals.append(jnp.broadcast_to((total - target_ref[r]) * grad_scale, (8, LANES)))
    pred_ref[...] = jnp.broadcast_to(found, (8, LANES))

    for half, out_ref in enumerate((keep_ref, send_ref)):

        @pl.loop(0, LANES // 8)
        def _(i):
            row = pl.multiple_of(i * 8, 8)
            rows_here = pl.ds(row + half * LANES, 8)
            for k in range(chunks):
                total = feat_ref[k, 0, rows_here, :] * residuals[0]
                for r in range(1, rows):
                    total = total + feat_ref[k, r, rows_here, :] * residuals[r]
                out_ref[k, pl.ds(row, 8), :] = total


def local(
    embeddings,
    sign_flips,
    gaussian,
    scales,
    phases,
    source_blocks,
    block_permutations,
    weights,
    targets,
):
    f32 = jnp.float32
    feat_size = lax.axis_size("feat")
    rows_size = lax.axis_size("rows")
    place = lax.axis_index("feat")
    core = lax.axis_index("rows")
    devices = feat_size * rows_size
    width = embeddings.shape[1]
    rows = embeddings.shape[0] // feat_size
    total_rows = embeddings.shape[0] * rows_size
    features = sign_flips.shape[0] * feat_size
    blocks = features // LANES
    mine = blocks // devices
    quarters = width // LANES
    chunks = blocks // CHUNK
    per_chunk = CHUNK // mine

    def half(values):
        parts = values.reshape((rows_size, values.shape[0] // rows_size) + values.shape[1:])
        return lax.dynamic_index_in_dim(parts, core, 0, False)

    def rows_of(*vectors):
        return jnp.concatenate([half(v) for v in vectors]).reshape(len(vectors), mine, LANES)

    positions = jnp.einsum(
        "bij,j->bi", half(block_permutations), jnp.arange(LANES).astype(jnp.bfloat16), preferred_element_type=f32
    )
    signs, gains = rows_of(sign_flips, gaussian)
    numbers = half(source_blocks).astype(f32)
    late = rows_of(
        scales * f32(4.0 / (2.0 * math.pi * features)),
        phases * f32(1.0 / (2.0 * math.pi)),
        weights * f32(1.0 / math.sqrt(features)),
    )
    bits = bits_of("feat")
    numbers = jnp.broadcast_to(jnp.pad(numbers, (0, LANES - mine))[None, :], (8, LANES))
    everything = [signs, positions, gains, *late, numbers]
    direct = mine == LANES and feat_size == chunks and rows_size == 2
    if direct:
        me = place * rows_size + core
        bits_a = bits[:-2] + [2, 1]
        bits_b = bits[:-2] + [1, 2]
    else:
        me = 0
        bits_a = bits_b = [1 << i for i in reversed(range(chunks.bit_length() - 1))]
        from_place = np.argsort([place_of(distance, bits_a) for distance in range(chunks)])
        whole = gather_ordered(jnp.concatenate(everything))
        numbers = whole[:, 6 * mine, :mine].reshape(chunks, 2, 1, LANES)
        numbers = jnp.broadcast_to(numbers, (chunks, 2, 8, LANES))[from_place]
        everything = [whole[:, i * mine : (i + 1) * mine].reshape(chunks, 2, LANES, LANES)[from_place] for i in range(6)]
        everything.append(numbers)
    signs, positions, gains, *late, numbers = everything

    per_half = LANES // quarters
    cut = LANES // 2
    shape = signs.shape
    signs = signs.reshape(shape[:-2] + (2, per_half // 2, quarters, LANES))
    signs = jnp.swapaxes(signs, -3, -2).reshape(shape)
    early = [jnp.concatenate([signs[..., :cut, :], numbers], axis=-2), signs[..., cut:, :]]
    middle = [positions, gains]
    late = [jnp.concatenate([x[..., part, :] for x in late], axis=-2) for part in (slice(0, cut), slice(cut, LANES))]

    emb = lax.dynamic_slice_in_dim(embeddings, place * rows, rows, 0)
    lane_signs = hadamard(LANES)
    emb = (emb.T.reshape(quarters, LANES, rows, 1) * jnp.asarray(lane_signs, jnp.bfloat16)[None, :, None, :]).reshape(
        width, rows * LANES
    )
    lane_matrix = jnp.asarray(np.concatenate([lane_signs] * 2, 0), jnp.bfloat16)
    block_matrix = jnp.asarray(np.concatenate([hadamard(CHUNK)] * 2, 1), jnp.bfloat16)
    about_me = jnp.stack([jnp.asarray(me, jnp.int32), (place * rows).astype(jnp.int32)])

    scalars = pl.BlockSpec(memory_space=pltpu.SMEM)
    vmem = pl.BlockSpec(memory_space=pltpu.VMEM)
    group = 2

    def first_of(begin, count, early, ready):
        shapes = [jax.ShapeDtypeStruct((count, rows, CHUNK, LANES), f32)]
        if begin == 0:
            shapes.append(jax.ShapeDtypeStruct((blocks // quarters, width), jnp.bfloat16))
            shapes.append(jax.ShapeDtypeStruct((width + LANES, rows * LANES), jnp.bfloat16))
        return pl.pallas_call(
            functools.partial(first_kernel, rows, begin, group, bits_a, bits_b),
            in_specs=[scalars] + [vmem] * (4 + len(ready)),
            out_specs=[vmem] * len(shapes),
            out_shape=shapes,
            compiler_params=pltpu.CompilerParams(vmem_limit_bytes=VMEM_MIX),
            cost_estimate=LITTLE,
            name="first",
        )(about_me, *early, *ready)

    def mix(begin, first, middle):
        count = first.shape[0]
        return pl.pallas_call(
            functools.partial(mix_kernel, rows, begin, group, bits_a, bits_b),
            in_specs=[scalars] + [vmem] * 11,
            out_specs=vmem,
            out_shape=jax.ShapeDtypeStruct(first.shape, f32),
            input_output_aliases={1: 0},
            scratch_shapes=[pltpu.VMEM((group, 2 * CHUNK, rows * LANES), jnp.bfloat16)],
            compiler_params=pltpu.CompilerParams(vmem_limit_bytes=VMEM_MIX),
            cost_estimate=LITTLE,
            name="mix",
        )(about_me, first, *middle, lane_matrix, block_matrix)

    cuts = [chunks * i // 4 for i in range(5)]
    if direct:
        orders = (bits_a, bits_b)

        def send(values, bit, *others):
            return swap(after(values, *others) if others else values, "feat", bit)

        def send_pair(pair, step, *others):
            return [send(x, b[step], *others) for x, b in zip(pair, orders)]

        def join(held, got, *others):
            return jnp.concatenate([held, after(got, *others) if others else got], axis=0)

        def join_pair(pair, got, *others):
            return [join(x, y, *others) for x, y in zip(pair, got)]

        def parted(held, pair):
            size = pair[0].shape[0]
            return [held[:, :size], held[:, size:]]

        def with_core(pair):
            return [y for x in pair for y in (x, swap(x, "rows", 1))]

        last = len(bits) - 1
        s_held, m_held, l_held = (jnp.concatenate(x, axis=0)[None] for x in (early, middle, late))
        m_step = None
        for i in range(last - 1):
            s_step = send(s_held, bits[i])
            m_next = send(m_held if m_step is None else join(m_held, m_step), bits[i], s_held)
            s_held = join(s_held, s_step)
            if m_step is not None:
                m_held = join(m_held, m_step)
            m_step = m_next
        s_pair = parted(s_held, early)
        s_step = send_pair(s_pair, last - 1)
        l_step = send(l_held, bits[0], s_held)
        m_held = join(m_held, m_step)
        m_pair = parted(m_held, middle)
        s_pair = join_pair(s_pair, s_step)
        s_step = send_pair(s_pair, last)
        m_step = send_pair(m_pair, last - 1, *s_pair)
        s_pair = join_pair(s_pair, s_step)
        s_all = with_core(s_pair)
        for i in range(1, last - 1):
            l_held = join(l_held, l_step)
            l_step = send(l_held, bits[i], m_held)
        m_pair = join_pair(m_pair, m_step)
        m_step = send_pair(m_pair, last, *s_pair)
        m_core = [swap(x, "rows", 1) for x in m_pair]
        first, *ready = first_of(0, cuts[1], s_all, [emb])
        first = [first]
        l_held = join(l_held, l_step)
        l_pair = parted(l_held, late)
        l_step = send_pair(l_pair, last - 1)
        s_all[0] = after(s_all[0], *l_pair)
        first += [first_of(cuts[i], cuts[i + 1] - cuts[i], s_all, ready)[0] for i in (1, 2)]
        l_pair = join_pair(l_pair, l_step, *first)
        l_step = send_pair(l_pair, last)
        l_core = [swap(x, "rows", 1) for x in l_pair]
        m_step = [after(x, *l_pair) for x in m_step]
        m_all = []
        for held, got, core_held in zip(m_pair, m_step, m_core):
            m_all += [held, got, core_held, swap(got, "rows", 1)]
        s_all[0] = after(s_all[0], *l_pair, *m_step)
        first.append(first_of(cuts[3], cuts[4] - cuts[3], s_all, ready)[0])
        m_all[0] = after(m_all[0], first[3])
        spread = []
        for k, x in zip(cuts, first):
            spread.append(mix(k, x, m_all))
            m_all[0] = after(m_all[0], spread[-1])
        l_step = [after(x, spread[-1]) for x in l_step]
        l_all = []
        for held, got, core_held in zip(l_pair, l_step, l_core):
            l_all += [held, got, core_held, swap(got, "rows", 1)]
    else:
        low, high = slice(0, chunks // 2), slice(chunks // 2, chunks)
        s_all = [part[:, c] for part in early for c in range(2)]
        m_all = [part[half, c] for part in middle for c in range(2) for half in (low, high)]
        l_all = [part[half, c] for part in late for c in range(2) for half in (low, high)]
        first, *ready = first_of(0, cuts[1], s_all, [emb])
        first = [first] + [first_of(cuts[i], cuts[i + 1] - cuts[i], s_all, ready)[0] for i in (1, 2, 3)]
        spread = [mix(k, x, m_all) for k, x in zip(cuts, first)]

    my_targets = lax.dynamic_slice_in_dim(targets, place * rows, rows, 0)
    found, keep, send = pl.pallas_call(
        functools.partial(
            head_kernel, rows, turn_sine_coefficients(3), 1.0 / math.sqrt(total_rows), bits_a, bits_b, len(spread)
        ),
        in_specs=[scalars, scalars] + [vmem] * (len(spread) + 8),
        out_specs=[vmem] * 3,
        out_shape=[
            jax.ShapeDtypeStruct((8, LANES), f32),
            jax.ShapeDtypeStruct((chunks, LANES, LANES), f32),
            jax.ShapeDtypeStruct((chunks, LANES, LANES), f32),
        ],
        scratch_shapes=[
            pltpu.VMEM((chunks, rows, CHUNK, LANES), f32),
            pltpu.VMEM((rows, 8, LANES), f32),
            pltpu.VMEM((chunks, 8, LANES), f32),
        ],
        compiler_params=pltpu.CompilerParams(vmem_limit_bytes=VMEM_HEAD),
        name="head",
    )(about_me, my_targets, *spread, *(l_all[i] for i in (0, 1, 4, 5, 2, 3, 6, 7)))

    if not direct:
        grads = jnp.stack([keep, send], 1).reshape(feat_size, rows_size, mine, LANES)
        grads = jnp.take(grads, jnp.arange(feat_size) ^ place, axis=0)
        keep = lax.dynamic_index_in_dim(grads, core, 1, False)
        send = lax.dynamic_index_in_dim(grads, core ^ 1, 1, False)
    feature_grad, found = scatter_sum(keep, send, found)
    return found[0], feature_grad.reshape(-1)


def solution(mesh):
    in_specs = (
        P("rows", None),
        P("feat"),
        P("feat"),
        P("feat"),
        P("feat"),
        P("feat"),
        P("feat", None, None),
        P("feat"),
        P("rows"),
    )
    out_specs = (P("rows"), P(("feat", "rows")))
    return jax.shard_map(local, mesh=mesh, in_specs=in_specs, out_specs=out_specs, check_vma=False)
```

```python
import functools
import math

import jax
import jax.numpy as jnp
import numpy as np
from jax import lax
from jax.experimental import pallas as pl
from jax.experimental.pallas import tpu as pltpu
from jax.sharding import PartitionSpec as P

LANES = 128
CHUNK = 256
BOTH = ("feat", "rows")
MIB = 1024 * 1024
VMEM_MIX = 16 * MIB
VMEM_HEAD = 20 * MIB
LITTLE = pl.CostEstimate(flops=1, bytes_accessed=1, transcendentals=0)


def hadamard(length):
    matrix = np.ones((1, 1), np.float32)
    while matrix.shape[0] < length:
        matrix = np.block([[matrix, matrix], [matrix, -matrix]])
    return matrix


def halves(values):
    high = values.astype(jnp.bfloat16)
    low = (values - high.astype(jnp.float32)).astype(jnp.bfloat16)
    return high, low


def swap(values, axis_name, bit):
    size = lax.axis_size(axis_name)
    return lax.ppermute(values, axis_name, [(i, i ^ bit) for i in range(size)])


def bits_of(axis_name):
    return [1 << i for i in reversed(range(lax.axis_size(axis_name).bit_length() - 1))]


def gather_ordered(piece):
    shape = piece.shape
    held = piece[None]
    for axis_name in BOTH:
        index = lax.axis_index(axis_name)
        for bit in bits_of(axis_name):
            other = swap(held, axis_name, bit)
            upper = (index & bit) != 0
            held = jnp.where(
                upper, jnp.stack([other, held], 1), jnp.stack([held, other], 1)
            ).reshape((-1,) + shape)
    return held


def after(value, *others):
    return lax.optimization_barrier((value, *others))[0]


def doubled(held, bit):
    return jnp.concatenate([held, swap(held, "feat", bit)], axis=0)


def place_of(distance, bits):
    place = 0
    for i, bit in enumerate(bits):
        place = place + (((distance >> (bit.bit_length() - 1)) & 1) << i)
    return place


def scatter_sum(keep, send, extra):
    terms = keep + swap(send, "rows", 1)
    bits = bits_of("feat")
    count, lanes = terms.shape[1:]
    terms = terms.reshape((2,) * len(bits) + (count, lanes))
    cut = count // 2
    parts = [terms[..., :cut, :], terms[..., cut:, :]]
    names = [list(bits), list(bits)]

    def exchange(part, left, bit, extra):
        axis = left.index(bit)
        left.remove(bit)
        keep = lax.index_in_dim(part, 0, axis, False)
        send = lax.index_in_dim(part, 1, axis, False).reshape(-1, lanes)
        if extra is None:
            return keep + swap(send, "feat", bit).reshape(keep.shape), None
        got = swap(jnp.concatenate([send, extra], axis=0), "feat", bit)
        return keep + got[: send.shape[0]].reshape(keep.shape), extra + got[send.shape[0] :]

    for bit_a, bit_b in ((1, 2), (2, 1)):
        parts[0], extra = exchange(parts[0], names[0], bit_a, extra)
        parts[1], _ = exchange(parts[1], names[1], bit_b, None)
    rest = jnp.concatenate(parts, axis=-2)
    for bit in list(reversed(names[0])):
        rest, extra = exchange(rest, names[0], bit, extra)
    return rest, extra


def odd_bits(value):
    value = value ^ (value >> 4)
    value = value ^ (value >> 2)
    return (value ^ (value >> 1)) & 1


def flip(bits):
    return (1 - 2 * (bits & 1)).astype(jnp.float32)


def prepare(bits_a, bits_b, a_own, a_other, b_own, b_other, emb_ref, sign_ref, wide_ref):
    f32 = jnp.float32
    bf16 = jnp.bfloat16
    chunks = a_own.shape[0]
    width = emb_ref.shape[0]
    quarters = width // LANES
    here = LANES // quarters
    few = here // 2
    order = [place_of(distance, bits_a) for distance in range(chunks)]

    for c, pair in enumerate(((a_own, b_own), (a_other, b_other))):
        for part, (ref, bits) in enumerate(zip(pair, (bits_a, bits_b))):
            for distance in range(chunks):
                top = (c * chunks + order[distance]) * here + part * few
                for q in range(quarters):
                    sign_ref[top : top + few, q * LANES : (q + 1) * LANES] = ref[
                        place_of(distance, bits), q * few : (q + 1) * few, :
                    ].astype(bf16)
    sums = jnp.dot(jnp.ones((16, sign_ref.shape[0]), bf16), sign_ref[...], preferred_element_type=f32)
    odd = 0.5 * sums - 2.0 * jnp.floor(0.25 * sums)
    row = lax.broadcasted_iota(jnp.int32, odd.shape, 0)
    column = lax.broadcasted_iota(jnp.int32, odd.shape, 1)
    odd = jnp.where((row < 2 * quarters) & ((row & (quarters - 1)) == column // LANES), 0.5 * odd, 0.0)
    rest = jnp.dot(odd.astype(bf16), emb_ref[...], preferred_element_type=f32)
    high = rest.astype(bf16).astype(f32)
    row = lax.broadcasted_iota(jnp.int32, rest.shape, 0)
    wide_ref[0:width, :] = emb_ref[...]
    wide_ref[width:, :] = jnp.zeros((LANES, wide_ref.shape[1]), bf16)
    wide_ref[width : width + 16, :] = jnp.where(row < quarters, high, rest - high).astype(bf16)


def first_kernel(rows, begin, group, bits_a, bits_b, me_ref, a_own, a_other, b_own, b_other, *refs):
    f32 = jnp.float32
    bf16 = jnp.bfloat16
    if begin == 0:
        emb_ref, out_ref, sign_ref, wide_ref = refs
        prepare(bits_a, bits_b, a_own, a_other, b_own, b_other, emb_ref, sign_ref, wide_ref)
    else:
        sign_ref, wide_ref, out_ref = refs
    here = sign_ref.shape[0] // (2 * a_own.shape[0])
    major_me = me_ref[0] * here
    low = here.bit_length() - 1
    lane = lax.broadcasted_iota(jnp.int32, (CHUNK, LANES), 1)

    @pl.loop(0, out_ref.shape[0] // group)
    def _(step):
        left = []
        for g in range(group):
            pa = place_of(begin + step * group + g, bits_a)
            columns = []
            for ref in (a_own, a_other):
                source = ref[pa, LANES // 2 : LANES // 2 + 1, :].astype(jnp.int32)
                major = source >> 2
                code = major & (here - 1)
                for i, bit in enumerate(bits_a):
                    code = code | (((major >> (low + bit.bit_length())) & 1) << (low + i))
                code = code | (((major >> low) & 1) << (low + len(bits_a)))
                code = code | ((source & 3) << 10) | ((lax.population_count(major & major_me) & 1) << 12)
                columns.append(jnp.broadcast_to(code.astype(f32), (LANES, LANES)).T)
            code = jnp.concatenate(columns, axis=0).astype(jnp.int32)
            tiles = [flip(lax.population_count(code & lane))]
            for shift in range(7, 10):
                turn = flip(code >> shift)
                tiles = tiles + [tile * turn for tile in tiles]
            signs = jnp.concatenate([tile.astype(bf16) for tile in tiles], axis=1)
            sums = jnp.dot(signs, sign_ref[...], preferred_element_type=f32)
            flip_me, flip_1, flip_2 = flip(code >> 12), flip(code >> 10), flip(code >> 11)
            turns = [flip_me, flip_me * flip_1, flip_me * flip_2, flip_me * flip_1 * flip_2]
            parts = [
                (jnp.floor(0.25 * sums[:, q * LANES : (q + 1) * LANES]) * turns[q]).astype(bf16)
                for q in range(4)
            ]
            tail = flip_me * jnp.where((lane & 1) != 0, flip_1, 1.0) * jnp.where((lane & 2) != 0, flip_2, 1.0)
            parts.append(jnp.where(lane < 8, tail, 0.0).astype(bf16))
            left.append(jnp.concatenate(parts, axis=1))
        first = jnp.dot(jnp.concatenate(left, axis=0), wide_ref[...], preferred_element_type=f32)
        for g in range(group):
            for r in range(rows):
                out_ref[step * group + g, r] = first[g * CHUNK : (g + 1) * CHUNK, r * LANES : (r + 1) * LANES]


def mix_kernel(rows, begin, group, bits_a, bits_b, me_ref, first_ref, *refs):
    a_refs, b_refs, (lane_ref, block_ref, out_ref, spread_ref) = refs[:4], refs[4:8], refs[8:]
    f32 = jnp.float32
    top = max(bits_a[-1], bits_b[-1])

    def piece(refs, core, chunk, within, bits):
        far = 1 if within & bits[-1] else 0
        return refs[2 * core + far][place_of(chunk, bits[:-1])]

    @pl.loop(0, out_ref.shape[0] // (2 * top))
    def _(step):
        for within in range(0, 2 * top, group):
            at = step * 2 * top + within
            orders = []
            gains = []
            for g in range(group):
                chunk = begin + at + g
                orders += [piece(a_refs, c, chunk, within + g, bits_a) for c in range(2)]
                gains += [
                    piece(b_refs, c, chunk, within + g, bits_b)
                    * (1 - 2 * odd_bits((2 * chunk + c) & me_ref[0])).astype(f32)
                    for c in range(2)
                ]
            order = jnp.concatenate(orders, axis=0).astype(jnp.int32)
            gain = jnp.concatenate(gains, axis=0)
            for r in range(rows):
                columns = slice(r * LANES, (r + 1) * LANES)
                first = jnp.concatenate([first_ref[at + g, r] for g in range(group)], axis=0)
                mixed = jnp.take_along_axis(first, order, axis=1) * gain
                across = jnp.dot(
                    jnp.concatenate(halves(mixed), axis=1), lane_ref[...], preferred_element_type=f32
                )
                high, low = halves(across)
                for g in range(group):
                    here = slice(g * CHUNK, (g + 1) * CHUNK)
                    spread_ref[g, 0:CHUNK, columns] = high[here]
                    spread_ref[g, CHUNK:, columns] = low[here]
            for g in range(group):
                result = jnp.dot(block_ref[...], spread_ref[g], preferred_element_type=f32)
                for r in range(rows):
                    out_ref[at + g, r] = result[:, r * LANES : (r + 1) * LANES]


def turn_sine_coefficients(degree):
    points = np.cos(np.pi * (np.arange(400) + 0.5) / 400)
    v = 0.125 + 0.125 * points
    fit = np.polynomial.chebyshev.Chebyshev.fit(
        v * v, np.sin(2 * np.pi * v) / v, degree, domain=[0, 0.0625], w=v
    )
    return [float(c) for c in fit.convert(kind=np.polynomial.Polynomial).coef]


def head_kernel(rows, coefs, grad_scale, bits_a, bits_b, parts, me_ref, target_ref, *refs):
    y_refs, late_refs, refs = refs[:parts], refs[parts : parts + 8], refs[parts + 8 :]
    pred_ref, keep_ref, send_ref, feat_ref, acc_ref, scale_ref = refs
    f32 = jnp.float32
    chunks = feat_ref.shape[0]
    cut = LANES // 2
    acc_ref[...] = jnp.zeros_like(acc_ref)

    for part in range(4):
        core, bits = part // 2, (bits_a, bits_b)[part % 2]
        near = late_refs[2 * part].shape[0]
        late = [late_refs[2 * part + place // near].at[place % near] for place in range(chunks)]
        turns_me = [
            (1 - 2 * (odd_bits((2 * k + core) & me_ref[0]) ^ odd_bits(me_ref[0]))).astype(f32)
            for k in range(chunks)
        ]

        @pl.loop(0, cut // 8)
        def _(i):
            row = pl.multiple_of(i * 8, 8)
            here = pl.ds(row + part * cut, 8)
            for k in range(chunks):
                scale_ref[k] = late[place_of(k, bits)][pl.ds(row, 8), :] * turns_me[k]
            for r in range(rows):
                values = [y_ref[k, r, here, :] for y_ref in y_refs for k in range(y_ref.shape[0])]
                width = 1
                while width < chunks:
                    for k in range(chunks):
                        if not k & width:
                            a, b = values[k], values[k | width]
                            values[k], values[k | width] = a + b, a - b
                    width *= 2
                acc = acc_ref[r]
                for k in range(chunks):
                    place = place_of(k, bits)
                    turns = values[k] * scale_ref[k] + late[place][pl.ds(row + cut, 8), :]
                    quarter = 0.25 - jnp.abs(turns - jnp.round(turns))
                    square = quarter * quarter
                    cosine = square * coefs[-1] + coefs[-2]
                    for c in coefs[-3::-1]:
                        cosine = cosine * square + c
                    cosine = cosine * quarter
                    feat_ref[k, r, here, :] = cosine
                    acc = acc + cosine * late[place][pl.ds(row + 2 * cut, 8), :]
                acc_ref[r] = acc

    residuals = []
    lane = lax.broadcasted_iota(jnp.int32, (1, LANES), 1)
    found = jnp.zeros((1, LANES), f32)
    for r in range(rows):
        total = jnp.sum(jnp.sum(acc_ref[r], axis=0, keepdims=True), axis=1, keepdims=True)
        found = found + jnp.where(lane == me_ref[1] + r, total, 0.0)
        residuals.append(jnp.broadcast_to((total - target_ref[r]) * grad_scale, (8, LANES)))
    pred_ref[...] = jnp.broadcast_to(found, (8, LANES))

    for half, out_ref in enumerate((keep_ref, send_ref)):

        @pl.loop(0, LANES // 8)
        def _(i):
            row = pl.multiple_of(i * 8, 8)
            rows_here = pl.ds(row + half * LANES, 8)
            for k in range(chunks):
                total = feat_ref[k, 0, rows_here, :] * residuals[0]
                for r in range(1, rows):
                    total = total + feat_ref[k, r, rows_here, :] * residuals[r]
                out_ref[k, pl.ds(row, 8), :] = total


def local(
    embeddings,
    sign_flips,
    gaussian,
    scales,
    phases,
    source_blocks,
    block_permutations,
    weights,
    targets,
):
    f32 = jnp.float32
    feat_size = lax.axis_size("feat")
    rows_size = lax.axis_size("rows")
    place = lax.axis_index("feat")
    core = lax.axis_index("rows")
    devices = feat_size * rows_size
    width = embeddings.shape[1]
    rows = embeddings.shape[0] // feat_size
    total_rows = embeddings.shape[0] * rows_size
    features = sign_flips.shape[0] * feat_size
    blocks = features // LANES
    mine = blocks // devices
    quarters = width // LANES
    chunks = blocks // CHUNK
    per_chunk = CHUNK // mine

    def half(values):
        size = values.shape[0] // rows_size
        return lax.dynamic_slice_in_dim(values, core * size, size, 0)

    def rows_of(*vectors):
        return jnp.concatenate([half(v) for v in vectors]).reshape(len(vectors), mine, LANES)

    positions = jnp.einsum(
        "bij,j->bi", half(block_permutations), jnp.arange(LANES).astype(jnp.bfloat16), preferred_element_type=f32
    )
    signs, gains = rows_of(sign_flips, gaussian)
    numbers = half(source_blocks).astype(f32)
    late = rows_of(
        scales * f32(4.0 / (2.0 * math.pi * features)),
        phases * f32(1.0 / (2.0 * math.pi)),
        weights * f32(1.0 / math.sqrt(features)),
    )
    bits = bits_of("feat")
    numbers = jnp.broadcast_to(jnp.pad(numbers, (0, LANES - mine))[None, :], (8, LANES))
    everything = [signs, positions, gains, *late, numbers]
    direct = mine == LANES and feat_size == chunks and rows_size == 2
    if direct:
        me = place * rows_size + core
        bits_a = bits[:-2] + [2, 1]
        bits_b = bits[:-2] + [1, 2]
    else:
        me = 0
        bits_a = bits_b = [1 << i for i in reversed(range(chunks.bit_length() - 1))]
        from_place = np.argsort([place_of(distance, bits_a) for distance in range(chunks)])
        whole = gather_ordered(jnp.concatenate(everything))
        numbers = whole[:, 6 * mine, :mine].reshape(chunks, 2, 1, LANES)
        numbers = jnp.broadcast_to(numbers, (chunks, 2, 8, LANES))[from_place]
        everything = [whole[:, i * mine : (i + 1) * mine].reshape(chunks, 2, LANES, LANES)[from_place] for i in range(6)]
        everything.append(numbers)
    signs, positions, gains, *late, numbers = everything

    per_half = LANES // quarters
    cut = LANES // 2
    shape = signs.shape
    signs = signs.reshape(shape[:-2] + (2, per_half // 2, quarters, LANES))
    signs = jnp.swapaxes(signs, -3, -2).reshape(shape)
    early = [jnp.concatenate([signs[..., :cut, :], numbers], axis=-2), signs[..., cut:, :]]
    middle = [positions, gains]
    late = [jnp.concatenate([x[..., part, :] for x in late], axis=-2) for part in (slice(0, cut), slice(cut, LANES))]

    emb = lax.dynamic_slice_in_dim(embeddings, place * rows, rows, 0)
    lane_signs = hadamard(LANES)
    emb = (emb.T.reshape(quarters, LANES, rows, 1) * jnp.asarray(lane_signs, jnp.bfloat16)[None, :, None, :]).reshape(
        width, rows * LANES
    )
    lane_matrix = jnp.asarray(np.concatenate([lane_signs] * 2, 0), jnp.bfloat16)
    block_matrix = jnp.asarray(np.concatenate([hadamard(CHUNK)] * 2, 1), jnp.bfloat16)
    about_me = jnp.stack([jnp.asarray(me, jnp.int32), (place * rows).astype(jnp.int32)])

    scalars = pl.BlockSpec(memory_space=pltpu.SMEM)
    vmem = pl.BlockSpec(memory_space=pltpu.VMEM)
    group = 2

    def first_of(begin, count, early, ready):
        shapes = [jax.ShapeDtypeStruct((count, rows, CHUNK, LANES), f32)]
        if begin == 0:
            shapes.append(jax.ShapeDtypeStruct((blocks // quarters, width), jnp.bfloat16))
            shapes.append(jax.ShapeDtypeStruct((width + LANES, rows * LANES), jnp.bfloat16))
        return pl.pallas_call(
            functools.partial(first_kernel, rows, begin, group, bits_a, bits_b),
            in_specs=[scalars] + [vmem] * (4 + len(ready)),
            out_specs=[vmem] * len(shapes),
            out_shape=shapes,
            compiler_params=pltpu.CompilerParams(vmem_limit_bytes=VMEM_MIX),
            cost_estimate=LITTLE,
            name="first",
        )(about_me, *early, *ready)

    def mix(begin, first, middle):
        count = first.shape[0]
        return pl.pallas_call(
            functools.partial(mix_kernel, rows, begin, group, bits_a, bits_b),
            in_specs=[scalars] + [vmem] * 11,
            out_specs=vmem,
            out_shape=jax.ShapeDtypeStruct(first.shape, f32),
            input_output_aliases={1: 0},
            scratch_shapes=[pltpu.VMEM((group, 2 * CHUNK, rows * LANES), jnp.bfloat16)],
            compiler_params=pltpu.CompilerParams(vmem_limit_bytes=VMEM_MIX),
            cost_estimate=LITTLE,
            name="mix",
        )(about_me, first, *middle, lane_matrix, block_matrix)

    cuts = [chunks * i // 4 for i in range(5)]
    if direct:
        orders = (bits_a, bits_b)

        def send(values, bit, *others):
            return swap(after(values, *others) if others else values, "feat", bit)

        def send_pair(pair, step, *others):
            return [send(x, b[step], *others) for x, b in zip(pair, orders)]

        def join(held, got, *others):
            return jnp.concatenate([held, after(got, *others) if others else got], axis=0)

        def join_pair(pair, got, *others):
            return [join(x, y, *others) for x, y in zip(pair, got)]

        def parted(held, pair):
            size = pair[0].shape[0]
            return [held[:, :size], held[:, size:]]

        def with_core(pair):
            return [y for x in pair for y in (x, swap(x, "rows", 1))]

        last = len(bits) - 1
        s_held, m_held, l_held = (jnp.concatenate(x, axis=0)[None] for x in (early, middle, late))
        m_step = None
        for i in range(last - 1):
            s_step = send(s_held, bits[i])
            m_next = send(m_held if m_step is None else join(m_held, m_step), bits[i], s_held)
            s_held = join(s_held, s_step)
            if m_step is not None:
                m_held = join(m_held, m_step)
            m_step = m_next
        s_pair = parted(s_held, early)
        s_step = send_pair(s_pair, last - 1)
        l_step = send(l_held, bits[0], s_held)
        m_held = join(m_held, m_step)
        m_pair = parted(m_held, middle)
        s_pair = join_pair(s_pair, s_step)
        s_step = send_pair(s_pair, last)
        m_step = send_pair(m_pair, last - 1, *s_pair)
        s_pair = join_pair(s_pair, s_step)
        s_all = with_core(s_pair)
        for i in range(1, last - 1):
            l_held = join(l_held, l_step)
            l_step = send(l_held, bits[i], m_held)
        m_pair = join_pair(m_pair, m_step)
        m_step = send_pair(m_pair, last, *s_pair)
        m_core = [swap(x, "rows", 1) for x in m_pair]
        first, *ready = first_of(0, cuts[1], s_all, [emb])
        first = [first]
        l_held = join(l_held, l_step)
        l_pair = parted(l_held, late)
        l_step = send_pair(l_pair, last - 1)
        s_all[0] = after(s_all[0], *l_pair)
        first += [first_of(cuts[i], cuts[i + 1] - cuts[i], s_all, ready)[0] for i in (1, 2)]
        l_pair = join_pair(l_pair, l_step, *first)
        l_step = send_pair(l_pair, last)
        l_core = [swap(x, "rows", 1) for x in l_pair]
        m_step = [after(x, *l_pair) for x in m_step]
        m_all = []
        for held, got, core_held in zip(m_pair, m_step, m_core):
            m_all += [held, got, core_held, swap(got, "rows", 1)]
        s_all[0] = after(s_all[0], *l_pair, *m_step)
        first.append(first_of(cuts[3], cuts[4] - cuts[3], s_all, ready)[0])
        m_all[0] = after(m_all[0], first[3])
        spread = []
        for k, x in zip(cuts, first):
            if k == cuts[3]:
                l_step = [after(x, spread[-1]) for x in l_step]
                m_all[0] = after(m_all[0], *l_step)
            spread.append(mix(k, x, m_all))
            m_all[0] = after(m_all[0], spread[-1])
        l_all = []
        for held, got, core_held in zip(l_pair, l_step, l_core):
            l_all += [held, got, core_held, swap(got, "rows", 1)]
    else:
        low, high = slice(0, chunks // 2), slice(chunks // 2, chunks)
        s_all = [part[:, c] for part in early for c in range(2)]
        m_all = [part[half, c] for part in middle for c in range(2) for half in (low, high)]
        l_all = [part[half, c] for part in late for c in range(2) for half in (low, high)]
        first, *ready = first_of(0, cuts[1], s_all, [emb])
        first = [first] + [first_of(cuts[i], cuts[i + 1] - cuts[i], s_all, ready)[0] for i in (1, 2, 3)]
        spread = [mix(k, x, m_all) for k, x in zip(cuts, first)]

    my_targets = lax.dynamic_slice_in_dim(targets, place * rows, rows, 0)
    found, keep, send = pl.pallas_call(
        functools.partial(
            head_kernel, rows, turn_sine_coefficients(3), 1.0 / math.sqrt(total_rows), bits_a, bits_b, len(spread)
        ),
        in_specs=[scalars, scalars] + [vmem] * (len(spread) + 8),
        out_specs=[vmem] * 3,
        out_shape=[
            jax.ShapeDtypeStruct((8, LANES), f32),
            jax.ShapeDtypeStruct((chunks, LANES, LANES), f32),
            jax.ShapeDtypeStruct((chunks, LANES, LANES), f32),
        ],
        scratch_shapes=[
            pltpu.VMEM((chunks, rows, CHUNK, LANES), f32),
            pltpu.VMEM((rows, 8, LANES), f32),
            pltpu.VMEM((chunks, 8, LANES), f32),
        ],
        compiler_params=pltpu.CompilerParams(vmem_limit_bytes=VMEM_HEAD),
        name="head",
    )(about_me, my_targets, *spread, *(l_all[i] for i in (0, 1, 4, 5, 2, 3, 6, 7)))

    if not direct:
        grads = jnp.stack([keep, send], 1).reshape(feat_size, rows_size, mine, LANES)
        grads = jnp.take(grads, jnp.arange(feat_size) ^ place, axis=0)
        keep = lax.dynamic_index_in_dim(grads, core, 1, False)
        send = lax.dynamic_index_in_dim(grads, core ^ 1, 1, False)
    feature_grad, found = scatter_sum(keep, send, found)
    return found[0], feature_grad.reshape(-1)


def solution(mesh):
    in_specs = (
        P("rows", None),
        P("feat"),
        P("feat"),
        P("feat"),
        P("feat"),
        P("feat"),
        P("feat", None, None),
        P("feat"),
        P("rows"),
    )
    out_specs = (P("rows"), P(("feat", "rows")))
    return jax.shard_map(local, mesh=mesh, in_specs=in_specs, out_specs=out_specs, check_vma=False)
```

```python
import functools
import math

import jax
import jax.numpy as jnp
import numpy as np
from jax import lax
from jax.experimental import pallas as pl
from jax.experimental.pallas import tpu as pltpu
from jax.sharding import PartitionSpec as P

LANES = 128
CHUNK = 256
BOTH = ("feat", "rows")
MIB = 1024 * 1024
VMEM_MIX = 16 * MIB
VMEM_HEAD = 20 * MIB
LITTLE = pl.CostEstimate(flops=1, bytes_accessed=1, transcendentals=0)


def hadamard(length):
    matrix = np.ones((1, 1), np.float32)
    while matrix.shape[0] < length:
        matrix = np.block([[matrix, matrix], [matrix, -matrix]])
    return matrix


def halves(values):
    high = values.astype(jnp.bfloat16)
    low = (values - high.astype(jnp.float32)).astype(jnp.bfloat16)
    return high, low


def swap(values, axis_name, bit):
    size = lax.axis_size(axis_name)
    return lax.ppermute(values, axis_name, [(i, i ^ bit) for i in range(size)])


def bits_of(axis_name):
    return [1 << i for i in reversed(range(lax.axis_size(axis_name).bit_length() - 1))]


def gather_ordered(piece):
    shape = piece.shape
    held = piece[None]
    for axis_name in BOTH:
        index = lax.axis_index(axis_name)
        for bit in bits_of(axis_name):
            other = swap(held, axis_name, bit)
            upper = (index & bit) != 0
            held = jnp.where(
                upper, jnp.stack([other, held], 1), jnp.stack([held, other], 1)
            ).reshape((-1,) + shape)
    return held


def after(value, *others):
    return lax.optimization_barrier((value, *others))[0]


def doubled(held, bit):
    return jnp.concatenate([held, swap(held, "feat", bit)], axis=0)


def place_of(distance, bits):
    place = 0
    for i, bit in enumerate(bits):
        place = place + (((distance >> (bit.bit_length() - 1)) & 1) << i)
    return place


def scatter_sum(keep, send, extra):
    terms = keep + swap(send, "rows", 1)
    bits = bits_of("feat")
    count, lanes = terms.shape[1:]
    terms = terms.reshape((2,) * len(bits) + (count, lanes))
    cut = count // 2
    parts = [terms[..., :cut, :], terms[..., cut:, :]]
    names = [list(bits), list(bits)]

    def exchange(part, left, bit, extra):
        axis = left.index(bit)
        left.remove(bit)
        keep = lax.index_in_dim(part, 0, axis, False)
        send = lax.index_in_dim(part, 1, axis, False).reshape(-1, lanes)
        if extra is None:
            return keep + swap(send, "feat", bit).reshape(keep.shape), None
        got = swap(jnp.concatenate([send, extra], axis=0), "feat", bit)
        return keep + got[: send.shape[0]].reshape(keep.shape), extra + got[send.shape[0] :]

    for bit_a, bit_b in ((1, 2), (2, 1)):
        parts[0], extra = exchange(parts[0], names[0], bit_a, extra)
        parts[1], _ = exchange(parts[1], names[1], bit_b, None)
    rest = jnp.concatenate(parts, axis=-2)
    for bit in list(reversed(names[0])):
        rest, extra = exchange(rest, names[0], bit, extra)
    return rest, extra


def odd_bits(value):
    value = value ^ (value >> 4)
    value = value ^ (value >> 2)
    return (value ^ (value >> 1)) & 1


def flip(bits):
    return (1 - 2 * (bits & 1)).astype(jnp.float32)


def prepare(bits_a, bits_b, a_own, a_other, b_own, b_other, emb_ref, sign_ref, wide_ref):
    f32 = jnp.float32
    bf16 = jnp.bfloat16
    chunks = a_own.shape[0]
    width = emb_ref.shape[0]
    quarters = width // LANES
    here = LANES // quarters
    few = here // 2
    order = [place_of(distance, bits_a) for distance in range(chunks)]

    for c, pair in enumerate(((a_own, b_own), (a_other, b_other))):
        for part, (ref, bits) in enumerate(zip(pair, (bits_a, bits_b))):
            for distance in range(chunks):
                top = (c * chunks + order[distance]) * here + part * few
                for q in range(quarters):
                    sign_ref[top : top + few, q * LANES : (q + 1) * LANES] = ref[
                        place_of(distance, bits), q * few : (q + 1) * few, :
                    ].astype(bf16)
    sums = jnp.dot(jnp.ones((16, sign_ref.shape[0]), bf16), sign_ref[...], preferred_element_type=f32)
    odd = 0.5 * sums - 2.0 * jnp.floor(0.25 * sums)
    row = lax.broadcasted_iota(jnp.int32, odd.shape, 0)
    column = lax.broadcasted_iota(jnp.int32, odd.shape, 1)
    odd = jnp.where((row < 2 * quarters) & ((row & (quarters - 1)) == column // LANES), 0.5 * odd, 0.0)
    rest = jnp.dot(odd.astype(bf16), emb_ref[...], preferred_element_type=f32)
    high = rest.astype(bf16).astype(f32)
    row = lax.broadcasted_iota(jnp.int32, rest.shape, 0)
    wide_ref[0:width, :] = emb_ref[...]
    wide_ref[width:, :] = jnp.zeros((LANES, wide_ref.shape[1]), bf16)
    wide_ref[width : width + 16, :] = jnp.where(row < quarters, high, rest - high).astype(bf16)


def first_kernel(rows, begin, group, bits_a, bits_b, me_ref, a_own, a_other, b_own, b_other, *refs):
    f32 = jnp.float32
    bf16 = jnp.bfloat16
    if begin == 0:
        emb_ref, out_ref, sign_ref, wide_ref = refs
        prepare(bits_a, bits_b, a_own, a_other, b_own, b_other, emb_ref, sign_ref, wide_ref)
    else:
        sign_ref, wide_ref, out_ref = refs
    here = sign_ref.shape[0] // (2 * a_own.shape[0])
    major_me = me_ref[0] * here
    low = here.bit_length() - 1
    lane = lax.broadcasted_iota(jnp.int32, (CHUNK, LANES), 1)

    @pl.loop(0, out_ref.shape[0] // group)
    def _(step):
        left = []
        for g in range(group):
            pa = place_of(begin + step * group + g, bits_a)
            columns = []
            for ref in (a_own, a_other):
                source = ref[pa, LANES // 2 : LANES // 2 + 1, :].astype(jnp.int32)
                major = source >> 2
                code = major & (here - 1)
                for i, bit in enumerate(bits_a):
                    code = code | (((major >> (low + bit.bit_length())) & 1) << (low + i))
                code = code | (((major >> low) & 1) << (low + len(bits_a)))
                code = code | ((source & 3) << 10) | ((lax.population_count(major & major_me) & 1) << 12)
                columns.append(jnp.broadcast_to(code.astype(f32), (LANES, LANES)).T)
            code = jnp.concatenate(columns, axis=0).astype(jnp.int32)
            tiles = [flip(lax.population_count(code & lane))]
            for shift in range(7, 10):
                turn = flip(code >> shift)
                tiles = tiles + [tile * turn for tile in tiles]
            signs = jnp.concatenate([tile.astype(bf16) for tile in tiles], axis=1)
            sums = jnp.dot(signs, sign_ref[...], preferred_element_type=f32)
            flip_me, flip_1, flip_2 = flip(code >> 12), flip(code >> 10), flip(code >> 11)
            turns = [flip_me, flip_me * flip_1, flip_me * flip_2, flip_me * flip_1 * flip_2]
            parts = [
                (jnp.floor(0.25 * sums[:, q * LANES : (q + 1) * LANES]) * turns[q]).astype(bf16)
                for q in range(4)
            ]
            tail = flip_me * jnp.where((lane & 1) != 0, flip_1, 1.0) * jnp.where((lane & 2) != 0, flip_2, 1.0)
            parts.append(jnp.where(lane < 8, tail, 0.0).astype(bf16))
            left.append(jnp.concatenate(parts, axis=1))
        first = jnp.dot(jnp.concatenate(left, axis=0), wide_ref[...], preferred_element_type=f32)
        for g in range(group):
            for r in range(rows):
                out_ref[step * group + g, r] = first[g * CHUNK : (g + 1) * CHUNK, r * LANES : (r + 1) * LANES]


def mix_kernel(rows, begin, group, bits_a, bits_b, me_ref, first_ref, *refs):
    a_refs, b_refs, (lane_ref, block_ref, out_ref, spread_ref) = refs[:4], refs[4:8], refs[8:]
    f32 = jnp.float32
    top = max(bits_a[-1], bits_b[-1])

    def piece(refs, core, chunk, within, bits):
        far = 1 if within & bits[-1] else 0
        return refs[2 * core + far][place_of(chunk, bits[:-1])]

    @pl.loop(0, out_ref.shape[0] // (2 * top))
    def _(step):
        for within in range(0, 2 * top, group):
            at = step * 2 * top + within
            orders = []
            gains = []
            for g in range(group):
                chunk = begin + at + g
                orders += [piece(a_refs, c, chunk, within + g, bits_a) for c in range(2)]
                gains += [
                    piece(b_refs, c, chunk, within + g, bits_b)
                    * (1 - 2 * odd_bits((2 * chunk + c) & me_ref[0])).astype(f32)
                    for c in range(2)
                ]
            order = jnp.concatenate(orders, axis=0).astype(jnp.int32)
            gain = jnp.concatenate(gains, axis=0)
            for r in range(rows):
                columns = slice(r * LANES, (r + 1) * LANES)
                first = jnp.concatenate([first_ref[at + g, r] for g in range(group)], axis=0)
                mixed = jnp.take_along_axis(first, order, axis=1) * gain
                across = jnp.dot(
                    jnp.concatenate(halves(mixed), axis=1), lane_ref[...], preferred_element_type=f32
                )
                high, low = halves(across)
                for g in range(group):
                    here = slice(g * CHUNK, (g + 1) * CHUNK)
                    spread_ref[g, 0:CHUNK, columns] = high[here]
                    spread_ref[g, CHUNK:, columns] = low[here]
            for g in range(group):
                result = jnp.dot(block_ref[...], spread_ref[g], preferred_element_type=f32)
                for r in range(rows):
                    out_ref[at + g, r] = result[:, r * LANES : (r + 1) * LANES]


def turn_sine_coefficients(degree):
    points = np.cos(np.pi * (np.arange(400) + 0.5) / 400)
    v = 0.125 + 0.125 * points
    fit = np.polynomial.chebyshev.Chebyshev.fit(
        v * v, np.sin(2 * np.pi * v) / v, degree, domain=[0, 0.0625], w=v
    )
    return [float(c) for c in fit.convert(kind=np.polynomial.Polynomial).coef]


def head_kernel(rows, coefs, grad_scale, bits_a, bits_b, parts, me_ref, target_ref, *refs):
    y_refs, late_refs, refs = refs[:parts], refs[parts : parts + 8], refs[parts + 8 :]
    pred_ref, keep_ref, send_ref, feat_ref, acc_ref, scale_ref = refs
    f32 = jnp.float32
    chunks = feat_ref.shape[0]
    cut = LANES // 2
    acc_ref[...] = jnp.zeros_like(acc_ref)

    for part in range(4):
        core, bits = part // 2, (bits_a, bits_b)[part % 2]
        near = late_refs[2 * part].shape[0]
        late = [late_refs[2 * part + place // near].at[place % near] for place in range(chunks)]
        turns_me = [
            (1 - 2 * (odd_bits((2 * k + core) & me_ref[0]) ^ odd_bits(me_ref[0]))).astype(f32)
            for k in range(chunks)
        ]

        @pl.loop(0, cut // 8)
        def _(i):
            row = pl.multiple_of(i * 8, 8)
            here = pl.ds(row + part * cut, 8)
            for k in range(chunks):
                scale_ref[k] = late[place_of(k, bits)][pl.ds(row, 8), :] * turns_me[k]
            for r in range(rows):
                values = [y_ref[k, r, here, :] for y_ref in y_refs for k in range(y_ref.shape[0])]
                width = 1
                while width < chunks:
                    for k in range(chunks):
                        if not k & width:
                            a, b = values[k], values[k | width]
                            values[k], values[k | width] = a + b, a - b
                    width *= 2
                accs = [acc_ref[r], None, None, None]
                for k in range(chunks):
                    place = place_of(k, bits)
                    turns = values[k] * scale_ref[k] + late[place][pl.ds(row + cut, 8), :]
                    quarter = 0.25 - jnp.abs(turns - jnp.round(turns))
                    square = quarter * quarter
                    cosine = square * coefs[-1] + coefs[-2]
                    for c in coefs[-3::-1]:
                        cosine = cosine * square + c
                    cosine = cosine * quarter
                    feat_ref[k, r, here, :] = cosine
                    term = cosine * late[place][pl.ds(row + 2 * cut, 8), :]
                    accs[k % 4] = term if accs[k % 4] is None else accs[k % 4] + term
                acc_ref[r] = (accs[0] + accs[1]) + (accs[2] + accs[3])

    residuals = []
    lane = lax.broadcasted_iota(jnp.int32, (1, LANES), 1)
    found = jnp.zeros((1, LANES), f32)
    for r in range(rows):
        total = jnp.sum(jnp.sum(acc_ref[r], axis=0, keepdims=True), axis=1, keepdims=True)
        found = found + jnp.where(lane == me_ref[1] + r, total, 0.0)
        residuals.append(jnp.broadcast_to((total - target_ref[r]) * grad_scale, (8, LANES)))
    pred_ref[...] = jnp.broadcast_to(found, (8, LANES))

    for half, out_ref in enumerate((keep_ref, send_ref)):

        @pl.loop(0, LANES // 8)
        def _(i):
            row = pl.multiple_of(i * 8, 8)
            rows_here = pl.ds(row + half * LANES, 8)
            for k in range(chunks):
                total = feat_ref[k, 0, rows_here, :] * residuals[0]
                for r in range(1, rows):
                    total = total + feat_ref[k, r, rows_here, :] * residuals[r]
                out_ref[k, pl.ds(row, 8), :] = total


def local(
    embeddings,
    sign_flips,
    gaussian,
    scales,
    phases,
    source_blocks,
    block_permutations,
    weights,
    targets,
):
    f32 = jnp.float32
    feat_size = lax.axis_size("feat")
    rows_size = lax.axis_size("rows")
    place = lax.axis_index("feat")
    core = lax.axis_index("rows")
    devices = feat_size * rows_size
    width = embeddings.shape[1]
    rows = embeddings.shape[0] // feat_size
    total_rows = embeddings.shape[0] * rows_size
    features = sign_flips.shape[0] * feat_size
    blocks = features // LANES
    mine = blocks // devices
    quarters = width // LANES
    chunks = blocks // CHUNK
    per_chunk = CHUNK // mine

    def half(values):
        size = values.shape[0] // rows_size
        return lax.dynamic_slice_in_dim(values, core * size, size, 0)

    def rows_of(*vectors):
        return jnp.concatenate([half(v) for v in vectors]).reshape(len(vectors), mine, LANES)

    positions = jnp.einsum(
        "bij,j->bi", half(block_permutations), jnp.arange(LANES).astype(jnp.bfloat16), preferred_element_type=f32
    )
    signs, gains = rows_of(sign_flips, gaussian)
    numbers = half(source_blocks).astype(f32)
    late = rows_of(
        scales * f32(4.0 / (2.0 * math.pi * features)),
        phases * f32(1.0 / (2.0 * math.pi)),
        weights * f32(1.0 / math.sqrt(features)),
    )
    bits = bits_of("feat")
    numbers = jnp.broadcast_to(jnp.pad(numbers, (0, LANES - mine))[None, :], (8, LANES))
    everything = [signs, positions, gains, *late, numbers]
    direct = mine == LANES and feat_size == chunks and rows_size == 2
    if direct:
        me = place * rows_size + core
        bits_a = bits[:-2] + [2, 1]
        bits_b = bits[:-2] + [1, 2]
    else:
        me = 0
        bits_a = bits_b = [1 << i for i in reversed(range(chunks.bit_length() - 1))]
        from_place = np.argsort([place_of(distance, bits_a) for distance in range(chunks)])
        whole = gather_ordered(jnp.concatenate(everything))
        numbers = whole[:, 6 * mine, :mine].reshape(chunks, 2, 1, LANES)
        numbers = jnp.broadcast_to(numbers, (chunks, 2, 8, LANES))[from_place]
        everything = [whole[:, i * mine : (i + 1) * mine].reshape(chunks, 2, LANES, LANES)[from_place] for i in range(6)]
        everything.append(numbers)
    signs, positions, gains, *late, numbers = everything

    per_half = LANES // quarters
    cut = LANES // 2
    shape = signs.shape
    signs = signs.reshape(shape[:-2] + (2, per_half // 2, quarters, LANES))
    signs = jnp.swapaxes(signs, -3, -2).reshape(shape)
    early = [jnp.concatenate([signs[..., :cut, :], numbers], axis=-2), signs[..., cut:, :]]
    middle = [positions, gains]
    late = [jnp.concatenate([x[..., part, :] for x in late], axis=-2) for part in (slice(0, cut), slice(cut, LANES))]

    emb = lax.dynamic_slice_in_dim(embeddings, place * rows, rows, 0)
    lane_signs = hadamard(LANES)
    emb = (emb.T.reshape(quarters, LANES, rows, 1) * jnp.asarray(lane_signs, jnp.bfloat16)[None, :, None, :]).reshape(
        width, rows * LANES
    )
    lane_matrix = jnp.asarray(np.concatenate([lane_signs] * 2, 0), jnp.bfloat16)
    block_matrix = jnp.asarray(np.concatenate([hadamard(CHUNK)] * 2, 1), jnp.bfloat16)
    about_me = jnp.stack([jnp.asarray(me, jnp.int32), (place * rows).astype(jnp.int32)])

    scalars = pl.BlockSpec(memory_space=pltpu.SMEM)
    vmem = pl.BlockSpec(memory_space=pltpu.VMEM)
    group = 2

    def first_of(begin, count, early, ready):
        shapes = [jax.ShapeDtypeStruct((count, rows, CHUNK, LANES), f32)]
        if begin == 0:
            shapes.append(jax.ShapeDtypeStruct((blocks // quarters, width), jnp.bfloat16))
            shapes.append(jax.ShapeDtypeStruct((width + LANES, rows * LANES), jnp.bfloat16))
        return pl.pallas_call(
            functools.partial(first_kernel, rows, begin, group, bits_a, bits_b),
            in_specs=[scalars] + [vmem] * (4 + len(ready)),
            out_specs=[vmem] * len(shapes),
            out_shape=shapes,
            compiler_params=pltpu.CompilerParams(vmem_limit_bytes=VMEM_MIX),
            cost_estimate=LITTLE,
            name="first",
        )(about_me, *early, *ready)

    def mix(begin, first, middle):
        count = first.shape[0]
        return pl.pallas_call(
            functools.partial(mix_kernel, rows, begin, group, bits_a, bits_b),
            in_specs=[scalars] + [vmem] * 11,
            out_specs=vmem,
            out_shape=jax.ShapeDtypeStruct(first.shape, f32),
            input_output_aliases={1: 0},
            scratch_shapes=[pltpu.VMEM((group, 2 * CHUNK, rows * LANES), jnp.bfloat16)],
            compiler_params=pltpu.CompilerParams(vmem_limit_bytes=VMEM_MIX),
            cost_estimate=LITTLE,
            name="mix",
        )(about_me, first, *middle, lane_matrix, block_matrix)

    cuts = [chunks * i // 4 for i in range(5)]
    if direct:
        orders = (bits_a, bits_b)

        def send(values, bit, *others):
            return swap(after(values, *others) if others else values, "feat", bit)

        def send_pair(pair, step, *others):
            return [send(x, b[step], *others) for x, b in zip(pair, orders)]

        def join(held, got, *others):
            return jnp.concatenate([held, after(got, *others) if others else got], axis=0)

        def join_pair(pair, got, *others):
            return [join(x, y, *others) for x, y in zip(pair, got)]

        def parted(held, pair):
            size = pair[0].shape[0]
            return [held[:, :size], held[:, size:]]

        def with_core(pair):
            return [y for x in pair for y in (x, swap(x, "rows", 1))]

        last = len(bits) - 1
        s_held, m_held, l_held = (jnp.concatenate(x, axis=0)[None] for x in (early, middle, late))
        m_step = None
        for i in range(last - 1):
            s_step = send(s_held, bits[i])
            m_next = send(m_held if m_step is None else join(m_held, m_step), bits[i], s_held)
            s_held = join(s_held, s_step)
            if m_step is not None:
                m_held = join(m_held, m_step)
            m_step = m_next
        s_pair = parted(s_held, early)
        s_step = send_pair(s_pair, last - 1)
        l_step = send(l_held, bits[0], s_held)
        m_held = join(m_held, m_step)
        m_pair = parted(m_held, middle)
        s_pair = join_pair(s_pair, s_step)
        s_step = send_pair(s_pair, last)
        m_step = send_pair(m_pair, last - 1)
        s_pair = join_pair(s_pair, s_step)
        s_all = with_core(s_pair)
        for i in range(1, last - 1):
            l_held = join(l_held, l_step)
            l_step = send(l_held, bits[i], m_held)
        m_pair = join_pair(m_pair, m_step)
        m_step = send_pair(m_pair, last, *s_pair)
        m_core = [swap(x, "rows", 1) for x in m_pair]
        first, *ready = first_of(0, cuts[1], s_all, [emb])
        first = [first]
        l_held = join(l_held, l_step)
        l_pair = parted(l_held, late)
        l_step = send_pair(l_pair, last - 1)
        s_all[0] = after(s_all[0], *l_pair)
        first += [first_of(cuts[i], cuts[i + 1] - cuts[i], s_all, ready)[0] for i in (1, 2)]
        l_pair = join_pair(l_pair, l_step, *first)
        l_step = send_pair(l_pair, last)
        l_core = [swap(x, "rows", 1) for x in l_pair]
        m_step = [after(x, *l_pair) for x in m_step]
        m_all = []
        for held, got, core_held in zip(m_pair, m_step, m_core):
            m_all += [held, got, core_held, swap(got, "rows", 1)]
        s_all[0] = after(s_all[0], *l_pair, *m_step)
        first.append(first_of(cuts[3], cuts[4] - cuts[3], s_all, ready)[0])
        m_all[0] = after(m_all[0], first[3])
        spread = []
        for k, x in zip(cuts, first):
            if k == cuts[3]:
                l_step = [after(x, spread[-1]) for x in l_step]
                m_all[0] = after(m_all[0], *l_step)
            spread.append(mix(k, x, m_all))
            m_all[0] = after(m_all[0], spread[-1])
        l_all = []
        for held, got, core_held in zip(l_pair, l_step, l_core):
            l_all += [held, got, core_held, swap(got, "rows", 1)]
    else:
        low, high = slice(0, chunks // 2), slice(chunks // 2, chunks)
        s_all = [part[:, c] for part in early for c in range(2)]
        m_all = [part[half, c] for part in middle for c in range(2) for half in (low, high)]
        l_all = [part[half, c] for part in late for c in range(2) for half in (low, high)]
        first, *ready = first_of(0, cuts[1], s_all, [emb])
        first = [first] + [first_of(cuts[i], cuts[i + 1] - cuts[i], s_all, ready)[0] for i in (1, 2, 3)]
        spread = [mix(k, x, m_all) for k, x in zip(cuts, first)]

    my_targets = lax.dynamic_slice_in_dim(targets, place * rows, rows, 0)
    found, keep, send = pl.pallas_call(
        functools.partial(
            head_kernel, rows, turn_sine_coefficients(3), 1.0 / math.sqrt(total_rows), bits_a, bits_b, len(spread)
        ),
        in_specs=[scalars, scalars] + [vmem] * (len(spread) + 8),
        out_specs=[vmem] * 3,
        out_shape=[
            jax.ShapeDtypeStruct((8, LANES), f32),
            jax.ShapeDtypeStruct((chunks, LANES, LANES), f32),
            jax.ShapeDtypeStruct((chunks, LANES, LANES), f32),
        ],
        scratch_shapes=[
            pltpu.VMEM((chunks, rows, CHUNK, LANES), f32),
            pltpu.VMEM((rows, 8, LANES), f32),
            pltpu.VMEM((chunks, 8, LANES), f32),
        ],
        compiler_params=pltpu.CompilerParams(vmem_limit_bytes=VMEM_HEAD),
        name="head",
    )(about_me, my_targets, *spread, *(l_all[i] for i in (0, 1, 4, 5, 2, 3, 6, 7)))

    if not direct:
        grads = jnp.stack([keep, send], 1).reshape(feat_size, rows_size, mine, LANES)
        grads = jnp.take(grads, jnp.arange(feat_size) ^ place, axis=0)
        keep = lax.dynamic_index_in_dim(grads, core, 1, False)
        send = lax.dynamic_index_in_dim(grads, core ^ 1, 1, False)
    feature_grad, found = scatter_sum(keep, send, found)
    return found[0], feature_grad.reshape(-1)


def solution(mesh):
    in_specs = (
        P("rows", None),
        P("feat"),
        P("feat"),
        P("feat"),
        P("feat"),
        P("feat"),
        P("feat", None, None),
        P("feat"),
        P("rows"),
    )
    out_specs = (P("rows"), P(("feat", "rows")))
    return jax.shard_map(local, mesh=mesh, in_specs=in_specs, out_specs=out_specs, check_vma=False)
```
